128 devices in a mesh: expert: 8 (over y, core), dp: 16 (over x, z).
Axes of the slice: x: 4, y: 4, z: 4, core: 2. Of those that a mesh axis runs over, the one named last changes fastest.
Arguments:
- tokens: bfloat16 [131072, 2048], P(('expert', 'dp')), may hold values from -6 to 6
- block_expert: int32 [1024, 1], P(('expert', 'dp')), may hold values from 0 to 7; in each aligned block of 8 rows (0 to 7, 8 to 15, ...) at most 2 rows name the same one
- gate_weight: bfloat16 [8, 2048, 768], P('expert', 'dp'), may hold values from -0.125 to 0.125
- up_weight: bfloat16 [8, 2048, 768], P('expert', 'dp'), may hold values from -0.125 to 0.125
- down_weight: bfloat16 [8, 768, 2048], P('expert', None, 'dp'), may hold values from -0.21875 to 0.21875
Outputs:
- r_factor: float32 [8, 768, 768], P('expert', 'dp')
- compressed_down: float32 [8, 768, 2048], P('expert', None, 'dp')
The draws below stay inside these ranges and needn't reach their ends.
Inputs may be any that keep to these rules, and one draw needn't show every extreme that they name: `block_expert`: among the 8 blocks of one device, at most 2 name the same expert, and in every draw some device has exactly 2 blocks for one expert.
All inputs are finite; a program needn't handle non-finite values.
Results may differ from the reference program's by a relative error of at most 0.0003.
Values may be sent and summed in bfloat16 or wider, within the bound.
A program may use at most 128 MiB of HBM per device.

```python
import math
import jax
import jax.numpy as jnp
import numpy as np
from jax import lax

D = 2048
FF = 768
BROWS = 128
BLK_DEV = 8
EXPERTS = 8
CAP = 2
NBLK = 1024
TOKENS = 131072
ROWS_AVG = 16384


def steps_of(own_key, shape, shards, least, largest):
    def one(dim, blocks):
        heights = jax.random.uniform(jax.random.fold_in(jax.random.fold_in(own_key, 6), dim), (blocks,), jnp.float32, least / len(shards), largest / len(shards))
        return jnp.repeat(jnp.exp(heights), shape[dim] // blocks).reshape((-1,) + (1,) * (len(shape) - dim - 1))

    level = one(*shards[0])
    for cut in shards[1:]:
        level = level * one(*cut)
    return level


def assign_block(stream_key, own, number, rows, amount, top, reach, lean):
    ranking = jax.random.permutation(stream_key, amount)
    crowded, usual = portions_of(amount, rows * top, reach, lean, True), portions_of(amount, rows * top, reach, lean, False)
    places = jnp.arange(amount)

    def named(tallies, rotation):
        used = int((tallies > 0).sum())
        fixed = max(1, used // 4)
        passed = fixed + (places - fixed + rotation * (used - fixed)) % max(1, amount - fixed)
        return jnp.zeros((amount,), jnp.int32).at[ranking[jnp.where(places < fixed, places, passed)]].set(jnp.asarray(tallies, jnp.int32))

    tallies = jnp.where(number % 4 == 0, named(crowded, number // 4), named(usual, number - number // 4 - 1))
    mixed = jax.random.permutation(jax.random.fold_in(own, 3), amount)
    donor, sink = mixed[0:amount // 2 * 2:2], mixed[1:amount // 2 * 2:2]
    margin = jnp.minimum(tallies[donor] - 1, reach - tallies[sink]) // 2
    margin = jnp.where((donor == ranking[0]) | (sink == ranking[0]) | (tallies[sink] == 0), 0, jnp.maximum(margin, 0))
    passed = jax.random.randint(jax.random.fold_in(own, 4), (amount // 2,), 0, 1 << 20) % (margin + 1)
    tallies = tallies.at[donor].add(-passed).at[sink].add(passed)
    members = jnp.searchsorted(jnp.cumsum(tallies), jnp.arange(rows * top), side="right").astype(jnp.int32)
    listing = members.reshape(top, rows).T
    listing = listing[jax.random.permutation(jax.random.fold_in(own, 1), rows)]
    rotation = jax.random.randint(jax.random.fold_in(own, 2), (rows, 1), 0, top)
    return jnp.take_along_axis(listing, (jnp.arange(top)[None, :] + rotation) % top, axis=1)


def portions_of(number_of, total, reach, slope, full):
    loads = [(1 << 20) // math.isqrt(standing ** slope) + 1 for standing in range(1, number_of + 1)]
    largest = reach if full else min(reach, max(-(-total // number_of), total * loads[0] // sum(loads)))
    least = 1 if total - largest >= number_of - 1 else 0
    counts, surplus = [largest] + [least] * (number_of - 1), total - largest - least * (number_of - 1)
    while surplus > 0:
        movable = [i for i in range(1, number_of) if counts[i] < largest] or [i for i in range(1, number_of) if counts[i] < reach]
        mass, left = sum([loads[i] for i in movable]), surplus
        for i in movable:
            extra = min(reach - counts[i], max(1, left * loads[i] // mass), surplus)
            counts[i] = counts[i] + extra
            surplus = surplus - extra
    return np.array(counts)


def gaussian(own_key, shape, scale, reach, pieces=(), held_as=jnp.bfloat16):
    gain = steps_of(own_key, shape, pieces, -0.22, 0.18) if pieces else 1.0
    entries = jax.random.normal(own_key, shape, jnp.float32) * scale * gain
    return jnp.minimum(jnp.maximum(entries, -reach), reach).astype(held_as)


def setup_inputs(seed: int = 0) -> dict:
    streams_of = jax.random.split(jax.random.key(seed), 6)
    tokens = gaussian(streams_of[0], (TOKENS, D), 1.0, 6.0, ((0, 128),))
    block_expert_keys = jax.random.split(jax.random.fold_in(streams_of[1], 1), NBLK // BLK_DEV)
    block_expert_turns = jax.random.permutation(jax.random.fold_in(streams_of[1], 3), NBLK // BLK_DEV)
    block_expert = jax.vmap(lambda own, number: assign_block(jax.random.fold_in(streams_of[1], 2), own, number, BLK_DEV, EXPERTS, 1, CAP, 2))(block_expert_keys, block_expert_turns).reshape((NBLK, 1))
    gate_weight = gaussian(streams_of[2], (EXPERTS, D, FF), D ** -0.5, 0.125, ((0, 8), (1, 16)))
    up_weight = gaussian(streams_of[3], (EXPERTS, D, FF), D ** -0.5, 0.125, ((0, 8), (1, 16)))
    down_weight = gaussian(streams_of[4], (EXPERTS, FF, D), FF ** -0.5, 0.21875, ((0, 8), (2, 16)))
    return dict(tokens=tokens, block_expert=block_expert, gate_weight=gate_weight, up_weight=up_weight, down_weight=down_weight)


damping = 0.05

def reference(tokens, block_expert, gate_weight, up_weight, down_weight):
    blocks = tokens.reshape(NBLK, BROWS, D)
    ids = block_expert[:, 0].astype(jnp.int32)

    def step(gram, item):
        block, expert_id = item
        gate = jnp.dot(block.astype(jnp.float32), gate_weight[expert_id].astype(jnp.float32), preferred_element_type=jnp.float32)
        upper_part = jnp.dot(block.astype(jnp.float32), up_weight[expert_id].astype(jnp.float32), preferred_element_type=jnp.float32)
        hidden = jax.nn.silu(gate) * upper_part
        term = jnp.dot(hidden.T, hidden, precision=lax.Precision.HIGHEST)
        return (gram.at[expert_id].add(term), None)
    gram, _ = lax.scan(step, jnp.zeros((EXPERTS, FF, FF), jnp.float32), (blocks, ids))
    gram = gram / float(ROWS_AVG) + damping * jnp.eye(FF, dtype=jnp.float32)[None]
    lower = jnp.linalg.cholesky(gram)
    r_factor = jnp.transpose(lower, (0, 2, 1))
    compressed = jnp.einsum('eij,ejk->eik', r_factor, down_weight.astype(jnp.float32), precision=lax.Precision.HIGHEST)
    return (r_factor, compressed)
```

```python
import jax
import jax.numpy as jnp
from jax import lax
from jax.experimental import pallas as pl
from jax.experimental.pallas import tpu as pltpu
from jax.sharding import PartitionSpec as P

BROWS = 128


damping = 0.05


HI = lax.Precision.HIGHEST


def lanes(v, k):
    return jnp.take_along_axis(v, jnp.full((8,128), k, jnp.int32), axis=1)
def subl(v, r):
    return jnp.broadcast_to(v[r:r+1, :], (8, 128))

def factor8(M):
    M = list(M)
    lane = lax.broadcasted_iota(jnp.int32, (8,128), 1)
    sub = lax.broadcasted_iota(jnp.int32, (8,128), 0)
    up, lo = [], []
    for q in range(16):
        k0 = 8*q
        C = {t: [lanes(M[t], k0+j) for j in range(8)] for t in range(q, 16)}
        E = list(C[q])
        own = (lane >= k0) & (lane < k0+8)
        ident = (lane == sub + k0).astype(jnp.float32)
        V = M[q]
        N = jnp.where(own, ident, M[q])
        F = N
        U = V
        dinv = jnp.zeros((8,128), jnp.float32)
        for j in range(8):
            d = subl(E[j], j)
            inv = 1.0 / d
            dinv = jnp.where(sub == j, inv, dinv)
            s = E[j] * inv
            fj = jnp.where(sub == j, 1.0 - inv, s)
            ff = jnp.where(sub > j, s, 0.0)
            for i in range(j+1, 8):
                E[i] = E[i] - fj * subl(E[i], j)
            N, F, U = N - fj * subl(N, j), F - ff * subl(F, j), U - ff * subl(U, j)
        rs = jnp.sqrt(dinv)
        U, F = U*rs, F*rs
        up.append(jnp.where(lane >= sub + k0, U, 0.0))
        lo.append(jnp.where(lane <= sub + k0, F, 0.0))
        G = [subl(N, j) for j in range(8)]
        for t in range(q+1, 16):
            base = jnp.where(own, 0.0, M[t])
            c = C[t]
            a = (c[0]*G[0] + c[1]*G[1]) + (c[2]*G[2] + c[3]*G[3])
            b = (c[4]*G[4] + c[5]*G[5]) + (c[6]*G[6] + c[7]*G[7])
            M[t] = base - (a + b)
    return up, lo

def kernel(me_ref, g_ref, w_ref, r_ref, p_ref, A, R, L):
    A[...] = g_ref[...]
    def body(kb, _):
        row = pl.multiple_of(kb*128, 128)
        blk = A[pl.ds(row,128), pl.ds(row,128)]
        up, lo = factor8([blk[8*t:8*t+8] for t in range(16)])
        zero = jnp.zeros((128,128), jnp.float32)
        for c in range(6):
            @pl.when(c < kb)
            def _(): R[pl.ds(row,128), c*128:(c+1)*128] = zero
        for t in range(16):
            R[pl.ds(row + 8*t, 8), pl.ds(row,128)] = up[t]
            L[8*t:8*t+8, :] = lo[t]
        for q in range(5):
            @pl.when(kb == q)
            def _():
                x = (q+1)*128
                P = jnp.dot(L[...], A[q*128:x, x:], precision=HI, preferred_element_type=jnp.float32)
                R[q*128:x, x:] = P
                for i in range(q+1, 6):
                    y = i*128
                    A[y:y+128, y:] -= lax.dot_general(P[:, y-x:y-x+128], P[:, y-x:], (((0,),(0,)),((),())), precision=HI, preferred_element_type=jnp.float32)
        return 0
    lax.fori_loop(0, 6, body, 0)
    r_ref[...] = R[pl.ds(pl.multiple_of(me_ref[0]*48, 8), 48), :]
    for i in range(6):
        y = i*128
        p_ref[y:y+128, :] = jnp.dot(R[y:y+128, y:], w_ref[y:, :].astype(jnp.float32), precision=HI, preferred_element_type=jnp.float32)

def chol(me, g, w):
    V = pl.BlockSpec(memory_space=pltpu.VMEM)
    return pl.pallas_call(kernel, out_shape=(jax.ShapeDtypeStruct((48,768),jnp.float32), jax.ShapeDtypeStruct((768,128),jnp.float32)),
        in_specs=[pl.BlockSpec(memory_space=pltpu.SMEM), V, V], out_specs=(V,V),
        scratch_shapes=[pltpu.VMEM((768,768),jnp.float32), pltpu.VMEM((768,768),jnp.float32), pltpu.VMEM((128,128),jnp.float32)],
        compiler_params=pltpu.CompilerParams(vmem_limit_bytes=40<<20))(me, g, w)


def fill_kernel(source_ref, block_ref, slot_ref):
    used = source_ref[pl.program_id(0)] < source_ref[source_ref.shape[0] - 1]

    @pl.when(used)
    def _():
        slot_ref[...] = block_ref[...]

    @pl.when(jnp.logical_not(used))
    def _():
        slot_ref[...] = jnp.zeros_like(slot_ref)


def fill_slots(source, blocks):
    count, rows, model = blocks.shape
    slots = source.shape[0]
    return pl.pallas_call(
        fill_kernel,
        out_shape=jax.ShapeDtypeStruct((slots, rows, model), blocks.dtype),
        grid_spec=pltpu.PrefetchScalarGridSpec(
            num_scalar_prefetch=1,
            grid=(slots,),
            in_specs=[pl.BlockSpec((1, rows, model), lambda s, src: (lax.rem(src[s], count), 0, 0))],
            out_specs=pl.BlockSpec((1, rows, model), lambda s, src: (s, 0, 0)),
        ),
    )(jnp.append(source, count), blocks)


def on_device(tokens, block_expert, gate_weight, up_weight, down_weight):
    n_expert = lax.axis_size("expert")
    n_data = lax.axis_size("dp")
    exp_local = gate_weight.shape[0]
    width = gate_weight.shape[2]
    model = tokens.shape[1]
    experts = exp_local * n_expert
    blk_count = block_expert.shape[0]
    capacity = max(2, 2 * blk_count // experts)
    rows_avg = blk_count * BROWS * n_data * n_expert // experts
    blocks = tokens.reshape(blk_count, BROWS, model)
    ids = block_expert[:, 0]
    positions = jnp.arange(blk_count, dtype=jnp.int32)
    same = ids[:, None] == ids[None, :]
    earlier = positions[None, :] < positions[:, None]
    ranks = jnp.sum((same & earlier).astype(jnp.int32), axis=1)
    slots = jnp.arange(experts * capacity, dtype=jnp.int32)
    match = (ids[None, :] == (slots // capacity)[:, None]) & (
        ranks[None, :] == (slots % capacity)[:, None]
    )
    found = jnp.sum(match.astype(jnp.int32), axis=1)
    source = jnp.sum(match.astype(jnp.int32) * positions[None, :], axis=1) + (1 - found) * blk_count
    outgoing = fill_slots(source, blocks).reshape(n_expert, exp_local, capacity, BROWS, model)
    arrived = lax.all_to_all(outgoing, "expert", split_axis=0, concat_axis=0, tiled=True)
    eye = jnp.eye(width, dtype=jnp.float32)
    rows = arrived[:, 0].reshape(-1, model)
    gate = jnp.dot(
        rows,
        lax.all_gather(gate_weight[0], "dp", axis=0, tiled=True),
        preferred_element_type=jnp.float32,
    )
    lifted = jnp.dot(
        rows,
        lax.all_gather(up_weight[0], "dp", axis=0, tiled=True),
        preferred_element_type=jnp.float32,
    )
    hidden = jax.nn.silu(gate) * lifted
    gram = jnp.dot(hidden.T, hidden, precision=lax.Precision.HIGHEST) / float(rows_avg)
    total = lax.psum(gram, "dp") + damping * eye
    me = lax.axis_index("dp").astype(jnp.int32).reshape(1)
    factor, product = chol(me, total, down_weight[0])
    return (factor[None], product[None])


def solution(mesh):
    placed = (
        P(("expert", "dp"), None),
        P(("expert", "dp"), None),
        P("expert", "dp", None),
        P("expert", "dp", None),
        P("expert", None, "dp"),
    )
    return jax.shard_map(
        on_device,
        mesh=mesh,
        in_specs=placed,
        out_specs=(P("expert", "dp", None), P("expert", None, "dp")),
        check_vma=False,
    )
```

```python
import functools

import jax
import jax.numpy as jnp
from jax import lax
from jax.experimental import pallas as pl
from jax.experimental.pallas import tpu as pltpu
from jax.sharding import PartitionSpec as P

BROWS = 128
HI = lax.Precision.HIGHEST
damping = 0.05
MESH = pl.DeviceIdType.MESH
PAIR = 2 * BROWS
MESSAGES = ((0, 0), (0, 1), (1, 0), (3, 0), (1, 1), (3, 1), (2, 0), (2, 1))


def gather_kernel(rows_avg, tok_ref, ids_ref, gate_ref, up_ref, sum_ref,
                  tok, send, got, wg, wu, hid, acc, pack, r1, q1, r2, q2,
                  local_sem, tok_ss, tok_rs, w_ss, w_rs, g_ss, g_rs):
    e, d = lax.axis_index("expert"), lax.axis_index("dp")
    y, c, x, z = e // 2, e % 2, d // 4, d % 4

    def at_y(dy, dc):
        return {"expert": ((y + dy) % 4) * 2 + (c + dc) % 2, "dp": d}

    def at_x(s):
        return {"expert": e, "dp": ((x + s) % 4) * 4 + z}

    def at_z(s):
        return {"expert": e, "dp": x * 4 + (z + s) % 4}

    bar = pltpu.get_barrier_semaphore()
    for m in MESSAGES[1:]:
        pl.semaphore_signal(bar, inc=1, device_id=at_y(*m), device_id_type=MESH)
    for s in (1, 2, 3):
        pl.semaphore_signal(bar, inc=1, device_id=at_x(s), device_id_type=MESH)
        pl.semaphore_signal(bar, inc=1, device_id=at_z(s), device_id_type=MESH)
    load = pltpu.make_async_copy(tok_ref, tok.at[pl.ds(0, 8)], local_sem.at[0])
    load.start()
    own_g = pltpu.make_async_copy(gate_ref, wg.at[x, z], local_sem.at[1])
    own_u = pltpu.make_async_copy(up_ref, wu.at[x, z], local_sem.at[2])
    own_g.start()
    own_u.start()
    pl.semaphore_wait(bar, 13)

    def remote(src, dst, ss, rs, to):
        copy = pltpu.make_async_remote_copy(src_ref=src, dst_ref=dst, send_sem=ss, recv_sem=rs, device_id=to, device_id_type=MESH)
        copy.start()
        return copy

    first = []
    for s in (1, 2, 3):
        first.append(remote(gate_ref, wg.at[x, z], w_ss.at[0, s - 1], w_rs.at[0, s - 1], at_x(s)))
        first.append(remote(up_ref, wu.at[x, z], w_ss.at[1, s - 1], w_rs.at[1, s - 1], at_z(s)))

    ids = [ids_ref[b] for b in range(8)]

    def slots(m):
        want = ((y + m[0]) % 4) * 2 + (c + m[1]) % 2
        one = two = jnp.int32(8)
        for b in range(7, -1, -1):
            hit = ids[b] == want
            two = jnp.where(hit, one, two)
            one = jnp.where(hit, jnp.int32(b), one)
        return one, two

    tok[8] = jnp.zeros_like(tok[8])
    load.wait()

    def post(u):
        for k, b in enumerate(slots(MESSAGES[u])):
            send[u - 1, k] = tok[b]
        return remote(send.at[u - 1], got.at[u], tok_ss.at[u - 1], tok_rs.at[u - 1], at_y(*MESSAGES[u]))

    sent = {u: post(u) for u in (2, 3, 4, 5)}
    sent[1] = post(1)
    for k, b in enumerate(slots(MESSAGES[0])):
        got[0, k] = tok[b]
    acc[...] = jnp.zeros_like(acc)

    own_g.wait()
    own_u.wait()
    for copy in first:
        copy.wait()
    second = []
    for s in (1, 2, 3):
        second.append(remote(wg.at[:, z], wg.at[:, z], w_ss.at[2, s - 1], w_rs.at[2, s - 1], at_z(s)))
        second.append(remote(wu.at[x], wu.at[x], w_ss.at[3, s - 1], w_rs.at[3, s - 1], at_x(s)))

    sent[2].wait()
    sent[3].wait()
    sent[6] = post(6)
    sent[1].wait()
    sent[4].wait()
    sent[5].wait()
    sent[7] = post(7)
    for copy in second:
        copy.wait()

    model, width = 16 * wg.shape[2], wg.shape[3]

    def unit(u, _):
        @pl.when(u == 6)
        def _():
            sent[6].wait()

        @pl.when(u == 7)
        def _():
            sent[7].wait()

        def part(n, _):
            cut = pl.ds(pl.multiple_of(n * 256, 256), 256)
            rows = got[u].reshape(PAIR, model)
            gate = jnp.dot(rows, wg[:, :, :, cut].reshape(model, 256), preferred_element_type=jnp.float32)
            lifted = jnp.dot(rows, wu[:, :, :, cut].reshape(model, 256), preferred_element_type=jnp.float32)
            hidden = gate / (1.0 + jnp.exp(-gate)) * lifted
            high = hidden.astype(jnp.bfloat16)
            low = (hidden - high.astype(jnp.float32)).astype(jnp.bfloat16)
            hid[0:256, cut] = high
            hid[256:512, cut] = high
            hid[512:768, cut] = low
            hid[768:1024, cut] = high
            return 0

        lax.fori_loop(0, width // 256, part, 0)
        for i in range(0, width, 256):
            acc[i:i + 256, i:] += lax.dot_general(
                hid[0:768, i:i + 256], hid[256:1024, i:], (((0,), (0,)), ((), ())), preferred_element_type=jnp.float32
            )
        return 0

    lax.fori_loop(0, 8, unit, 0)

    for i in range(3):
        w = width - 128 * i
        top, low = i * 128, (5 - i) * 128
        pack[top:top + 128, 0:w] = acc[top:top + 128, top:] * (1.0 / rows_avg)
        pack[top:top + 128, w:] = acc[low:low + 128, low:] * (1.0 / rows_avg)

    A, B = pl.ds(0, 512), pl.ds(512, 384)

    def at(r, n):
        return pl.ds(pl.multiple_of(r, 8), n)

    copies = []
    for s in (1, 2, 3):
        tx, tz = (x + s) % 4, (z + s) % 4
        copies.append(remote(pack.at[at(tx * 96, 96), A], r1.at[s - 1, :, A], g_ss.at[0, s - 1], g_rs.at[0, s - 1], at_x(s)))
        copies.append(remote(pack.at[at(tz * 96, 96), B], r1.at[s - 1, :, B], g_ss.at[1, s - 1], g_rs.at[1, s - 1], at_z(s)))
    for copy in copies:
        copy.wait()
    q1[:, A] = (pack[at(x * 96, 96), A] + r1[0, :, A]) + (r1[1, :, A] + r1[2, :, A])
    q1[:, B] = (pack[at(z * 96, 96), B] + r1[0, :, B]) + (r1[1, :, B] + r1[2, :, B])
    copies = []
    for s in (1, 2, 3):
        tx, tz = (x + s) % 4, (z + s) % 4
        copies.append(remote(q1.at[at(tz * 24, 24), A], r2.at[s - 1, :, A], g_ss.at[2, s - 1], g_rs.at[2, s - 1], at_z(s)))
        copies.append(remote(q1.at[at(tx * 24, 24), B], r2.at[s - 1, :, B], g_ss.at[3, s - 1], g_rs.at[3, s - 1], at_x(s)))
    for copy in copies:
        copy.wait()
    mine_a, mine_b = at(x * 96 + z * 24, 24), at(z * 96 + x * 24, 24)
    q2[mine_a, A] = (q1[at(z * 24, 24), A] + r2[0, :, A]) + (r2[1, :, A] + r2[2, :, A])
    q2[mine_b, B] = (q1[at(x * 24, 24), B] + r2[0, :, B]) + (r2[1, :, B] + r2[2, :, B])
    copies = []
    for s in (1, 2, 3):
        copies.append(remote(q2.at[mine_a, A], q2.at[mine_a, A], g_ss.at[4, s - 1], g_rs.at[4, s - 1], at_z(s)))
        copies.append(remote(q2.at[mine_b, B], q2.at[mine_b, B], g_ss.at[5, s - 1], g_rs.at[5, s - 1], at_x(s)))
    for copy in copies:
        copy.wait()
    row_a, row_b = at(x * 96, 96), at(z * 96, 96)
    copies = []
    for s in (1, 2, 3):
        copies.append(remote(q2.at[row_a, A], q2.at[row_a, A], g_ss.at[6, s - 1], g_rs.at[6, s - 1], at_x(s)))
        copies.append(remote(q2.at[row_b, B], q2.at[row_b, B], g_ss.at[7, s - 1], g_rs.at[7, s - 1], at_z(s)))
    for copy in copies:
        copy.wait()
    sum_ref[...] = q2[...]


def gram_sums(tokens, ids, gate, up, rows_avg):
    model, width = tokens.shape[1], gate.shape[1]
    any_ = pl.BlockSpec(memory_space=pl.ANY)
    bf, f32, dma = jnp.bfloat16, jnp.float32, pltpu.SemaphoreType.DMA
    return pl.pallas_call(
        functools.partial(gather_kernel, float(rows_avg)),
        out_shape=jax.ShapeDtypeStruct((width // 2, width + 128), f32),
        in_specs=[any_, pl.BlockSpec(memory_space=pltpu.SMEM), any_, any_],
        out_specs=pl.BlockSpec(memory_space=pltpu.VMEM),
        scratch_shapes=[
            pltpu.VMEM((9, BROWS, model), bf),
            pltpu.VMEM((7, 2, BROWS, model), bf),
            pltpu.VMEM((8, 2, BROWS, model), bf),
            pltpu.VMEM((4, 4, model // 16, width), bf),
            pltpu.VMEM((4, 4, model // 16, width), bf),
            pltpu.VMEM((4 * PAIR, width), bf),
            pltpu.VMEM((width, width), f32),
            pltpu.VMEM((width // 2, width + 128), f32),
            pltpu.VMEM((3, width // 8, width + 128), f32),
            pltpu.VMEM((width // 8, width + 128), f32),
            pltpu.VMEM((3, width // 32, width + 128), f32),
            pltpu.VMEM((width // 2, width + 128), f32),
            dma((3,)), dma((7,)), dma((7,)), dma((4, 3)), dma((4, 3)), dma((8, 3)), dma((8, 3)),
        ],
        compiler_params=pltpu.CompilerParams(collective_id=1, has_side_effects=True, vmem_limit_bytes=56 << 20),
    )(tokens.reshape(8, BROWS, model), ids, gate, up)


def lanes(v, k):
    return jnp.take_along_axis(v, jnp.full((8,128), k, jnp.int32), axis=1)
def subl(v, r):
    return jnp.broadcast_to(v[r:r+1, :], (8, 128))

def factor8(M):
    M = list(M)
    lane = lax.broadcasted_iota(jnp.int32, (8,128), 1)
    sub = lax.broadcasted_iota(jnp.int32, (8,128), 0)
    up, lo = [], []
    for q in range(16):
        k0 = 8*q
        C = {t: [lanes(M[t], k0+j) for j in range(8)] for t in range(q, 16)}
        E = list(C[q])
        own = (lane >= k0) & (lane < k0+8)
        ident = (lane == sub + k0).astype(jnp.float32)
        V = M[q]
        N = jnp.where(own, ident, M[q])
        F = N
        U = V
        dinv = jnp.zeros((8,128), jnp.float32)
        for j in range(8):
            d = subl(E[j], j)
            inv = 1.0 / d
            dinv = jnp.where(sub == j, inv, dinv)
            s = E[j] * inv
            fj = jnp.where(sub == j, 1.0 - inv, s)
            ff = jnp.where(sub > j, s, 0.0)
            for i in range(j+1, 8):
                E[i] = E[i] - fj * subl(E[i], j)
            N, F, U = N - fj * subl(N, j), F - ff * subl(F, j), U - ff * subl(U, j)
        rs = jnp.sqrt(dinv)
        U, F = U*rs, F*rs
        up.append(jnp.where(lane >= sub + k0, U, 0.0))
        lo.append(jnp.where(lane <= sub + k0, F, 0.0))
        G = [subl(N, j) for j in range(8)]
        for t in range(q+1, 16):
            base = jnp.where(own, 0.0, M[t])
            c = C[t]
            a = (c[0]*G[0] + c[1]*G[1]) + (c[2]*G[2] + c[3]*G[3])
            b = (c[4]*G[4] + c[5]*G[5]) + (c[6]*G[6] + c[7]*G[7])
            M[t] = base - (a + b)
    return up, lo

def kernel(me_ref, g_ref, w_ref, r_ref, p_ref, A, R, L):
    same = lax.broadcasted_iota(jnp.int32, (128, 128), 0) == lax.broadcasted_iota(jnp.int32, (128, 128), 1)
    for i in range(6):
        top, y, w = min(i, 5 - i) * 128, i * 128, 768 - 128 * i
        lead = 0 if i < 3 else 896 - w
        A[y:y+128, y:y+128] = g_ref[top:top+128, lead:lead+128] + jnp.where(same, damping, 0.0)
        if w > 128:
            A[y:y+128, y+128:] = g_ref[top:top+128, lead+128:lead+w]
    def body(kb, _):
        row = pl.multiple_of(kb*128, 128)
        blk = A[pl.ds(row,128), pl.ds(row,128)]
        up, lo = factor8([blk[8*t:8*t+8] for t in range(16)])
        zero = jnp.zeros((128,128), jnp.float32)
        for c in range(6):
            @pl.when(c < kb)
            def _(): R[pl.ds(row,128), c*128:(c+1)*128] = zero
        for t in range(16):
            R[pl.ds(row + 8*t, 8), pl.ds(row,128)] = up[t]
            L[8*t:8*t+8, :] = lo[t]
        for q in range(5):
            @pl.when(kb == q)
            def _():
                x = (q+1)*128
                P = jnp.dot(L[...], A[q*128:x, x:], precision=HI, preferred_element_type=jnp.float32)
                R[q*128:x, x:] = P
                for i in range(q+1, 6):
                    y = i*128
                    A[y:y+128, y:] -= lax.dot_general(P[:, y-x:y-x+128], P[:, y-x:], (((0,),(0,)),((),())), precision=HI, preferred_element_type=jnp.float32)
        return 0
    lax.fori_loop(0, 6, body, 0)
    r_ref[...] = R[pl.ds(pl.multiple_of(me_ref[0]*48, 8), 48), :]
    for i in range(6):
        y = i*128
        p_ref[y:y+128, :] = jnp.dot(R[y:y+128, y:], w_ref[y:, :].astype(jnp.float32), precision=HI, preferred_element_type=jnp.float32)

def chol(me, g, w):
    V = pl.BlockSpec(memory_space=pltpu.VMEM)
    return pl.pallas_call(kernel, out_shape=(jax.ShapeDtypeStruct((48,768),jnp.float32), jax.ShapeDtypeStruct((768,128),jnp.float32)),
        in_specs=[pl.BlockSpec(memory_space=pltpu.SMEM), V, V], out_specs=(V,V),
        scratch_shapes=[pltpu.VMEM((768,768),jnp.float32), pltpu.VMEM((768,768),jnp.float32), pltpu.VMEM((128,128),jnp.float32)],
        compiler_params=pltpu.CompilerParams(vmem_limit_bytes=40<<20))(me, g, w)


def on_device(tokens, block_expert, gate_weight, up_weight, down_weight):
    rows_avg = tokens.shape[0] * lax.axis_size("expert") * lax.axis_size("dp") // lax.axis_size("expert")
    total = gram_sums(tokens, block_expert[:, 0], gate_weight[0], up_weight[0], rows_avg)
    me = lax.axis_index("dp").astype(jnp.int32).reshape(1)
    factor, product = chol(me, total, down_weight[0])
    return (factor[None], product[None])


def solution(mesh):
    placed = (
        P(("expert", "dp"), None),
        P(("expert", "dp"), None),
        P("expert", "dp", None),
        P("expert", "dp", None),
        P("expert", None, "dp"),
    )
    return jax.shard_map(
        on_device,
        mesh=mesh,
        in_specs=placed,
        out_specs=(P("expert", "dp", None), P("expert", None, "dp")),
        check_vma=False,
    )
```

```python
import functools

import jax
import jax.numpy as jnp
from jax import lax
from jax.experimental import pallas as pl
from jax.experimental.pallas import tpu as pltpu
from jax.sharding import PartitionSpec as P

BROWS = 128
HI = lax.Precision.HIGHEST
damping = 0.05
MESH = pl.DeviceIdType.MESH
PAIR = 2 * BROWS
NEAR = ((0, 1, 0, 1, 0), (0, 1, 1, 1, 1))
STEPS = (
    ((2, 0, 0, 2, 0),),
    ((2, 0, 1, 2, 1),),
    ((2, 1, 0, 3, 0),),
    ((2, 1, 1, 3, 1),),
    ((1, 0, 0, 4, 0), (3, 0, 0, 4, 1)),
    ((1, 0, 1, 5, 0), (3, 0, 1, 5, 1)),
    ((1, 1, 0, 6, 0), (3, 1, 0, 6, 1)),
    ((1, 1, 1, 7, 0), (3, 1, 1, 7, 1)),
)
AHEAD = 3


def whole_kernel(rows_avg, tok_ref, ids_ref, gate_ref, up_ref, down_ref, r_ref, p_ref,
                  tok, send, got, wg, wu, hid, acc, pack, r1, q1, r2, q2, down, A, R, L,
                  local_sem, tok_ss, tok_rs, w_ss, w_rs, g_ss, g_rs):
    e, d = lax.axis_index("expert"), lax.axis_index("dp")
    y, c, x, z = e // 2, e % 2, d // 4, d % 4

    def at_y(dy, dc):
        return {"expert": ((y + dy) % 4) * 2 + (c + dc) % 2, "dp": d}

    def at_x(s):
        return {"expert": e, "dp": ((x + s) % 4) * 4 + z}

    def at_z(s):
        return {"expert": e, "dp": x * 4 + (z + s) % 4}

    bar = pltpu.get_barrier_semaphore()
    for dy, dc in ((0, 1), (1, 0), (1, 1), (2, 0), (2, 1), (3, 0), (3, 1)):
        pl.semaphore_signal(bar, inc=1, device_id=at_y(dy, dc), device_id_type=MESH)
    for s in (1, 2, 3):
        pl.semaphore_signal(bar, inc=1, device_id=at_x(s), device_id_type=MESH)
        pl.semaphore_signal(bar, inc=1, device_id=at_z(s), device_id_type=MESH)
    load = pltpu.make_async_copy(tok_ref, tok.at[pl.ds(0, 8)], local_sem.at[0])
    load.start()
    own_g = pltpu.make_async_copy(gate_ref, wg.at[x, z], local_sem.at[1])
    own_u = pltpu.make_async_copy(up_ref, wu.at[x, z], local_sem.at[2])
    own_d = pltpu.make_async_copy(down_ref, down, local_sem.at[3])
    own_d.start()
    own_g.start()
    own_u.start()
    pl.semaphore_wait(bar, 13)

    def remote(src, dst, ss, rs, to):
        copy = pltpu.make_async_remote_copy(src_ref=src, dst_ref=dst, send_sem=ss, recv_sem=rs, device_id=to, device_id_type=MESH)
        copy.start()
        return copy

    first = []
    for s in (1, 2, 3):
        first.append(remote(gate_ref, wg.at[x, z], w_ss.at[0, s - 1], w_rs.at[0, s - 1], at_x(s)))
        first.append(remote(up_ref, wu.at[x, z], w_ss.at[1, s - 1], w_rs.at[1, s - 1], at_z(s)))

    ids = [ids_ref[b] for b in range(8)]

    def slot(dy, dc, second):
        want = ((y + dy) % 4) * 2 + (c + dc) % 2
        one = two = jnp.int32(8)
        for b in range(7, -1, -1):
            hit = ids[b] == want
            two = jnp.where(hit, one, two)
            one = jnp.where(hit, jnp.int32(b), one)
        return two if second else one

    tok[8] = jnp.zeros_like(tok[8])
    load.wait()

    def block_copy(dy, dc, second, u, half):
        return pltpu.make_async_remote_copy(
            src_ref=send.at[u, half], dst_ref=got.at[u, half], send_sem=tok_ss.at[u, half], recv_sem=tok_rs.at[u, half],
            device_id=at_y(dy, dc), device_id_type=MESH,
        )

    def post(blocks):
        for b in blocks:
            send[b[3], b[4]] = tok[slot(*b[:3])]
            block_copy(*b).start()

    def sent(blocks):
        for b in blocks:
            block_copy(*b).wait_send()

    for n in range(AHEAD):
        post(STEPS[n])
    post(NEAR)
    for k in range(2):
        got[0, k] = tok[slot(0, 0, k)]
    acc[...] = jnp.zeros_like(acc)
    A[...] = jnp.zeros_like(A)
    R[...] = jnp.zeros_like(R)

    own_g.wait()
    own_u.wait()
    for copy in first:
        copy.wait()
    second = []
    for s in (1, 2, 3):
        second.append(remote(wg.at[:, z], wg.at[:, z], w_ss.at[2, s - 1], w_rs.at[2, s - 1], at_z(s)))
        second.append(remote(wu.at[x], wu.at[x], w_ss.at[3, s - 1], w_rs.at[3, s - 1], at_x(s)))
    for n in range(AHEAD, 6):
        sent(STEPS[n - AHEAD])
        post(STEPS[n])
    sent(NEAR)
    for copy in second:
        copy.wait()

    model, width = 16 * wg.shape[2], wg.shape[3]

    def unit(u, _):
        for n in (6, 7):
            @pl.when(u == n - 3)
            def _():
                sent(STEPS[n - AHEAD])
                post(STEPS[n])

        for blocks in (NEAR, STEPS[0] + STEPS[1], STEPS[2] + STEPS[3]) + STEPS[4:]:
            @pl.when(u == blocks[0][3])
            def _():
                for b in blocks:
                    block_copy(*b).wait_recv()

        def part(n, _):
            cut = pl.ds(pl.multiple_of(n * 256, 256), 256)
            rows = got[u].reshape(PAIR, model)
            gate = jnp.dot(rows, wg[:, :, :, cut].reshape(model, 256), preferred_element_type=jnp.float32)
            lifted = jnp.dot(rows, wu[:, :, :, cut].reshape(model, 256), preferred_element_type=jnp.float32)
            hidden = gate / (1.0 + jnp.exp(-gate)) * lifted
            high = hidden.astype(jnp.bfloat16)
            low = (hidden - high.astype(jnp.float32)).astype(jnp.bfloat16)
            hid[0:256, cut] = high
            hid[256:512, cut] = high
            hid[512:768, cut] = low
            hid[768:1024, cut] = high
            return 0

        lax.fori_loop(0, width // 256, part, 0)
        for i in range(0, width, 256):
            acc[i:i + 256, i:] += lax.dot_general(
                hid[0:768, i:i + 256], hid[256:1024, i:], (((0,), (0,)), ((), ())), preferred_element_type=jnp.float32
            )
        return 0

    lax.fori_loop(0, 8, unit, 0)
    for n in range(8 - AHEAD, 8):
        sent(STEPS[n])

    def fill(i):
        w = width - 128 * i
        top, low = i * 128, (5 - i) * 128
        pack[i, :, 0:w] = acc[top:top + 128, top:] * (1.0 / rows_avg)
        pack[i, :, w:] = acc[low:low + 128, low:] * (1.0 / rows_avg)

    CA, CB = pl.ds(0, 512), pl.ds(512, 384)

    def at(r, n):
        return pl.ds(pl.multiple_of(r, 8), n)

    mine_a, mine_b = at(x * 32 + z * 8, 8), at(z * 32 + x * 8, 8)

    def stage(i, k):
        out = []
        for s in (1, 2, 3):
            tx, tz = (x + s) % 4, (z + s) % 4
            if k == 0:
                a = pack.at[i, at(tx * 32, 32), CA], r1.at[i, s - 1, :, CA], at_x(s)
                b = pack.at[i, at(tz * 32, 32), CB], r1.at[i, s - 1, :, CB], at_z(s)
            elif k == 1:
                a = q1.at[i, at(tz * 8, 8), CA], r2.at[i, s - 1, :, CA], at_z(s)
                b = q1.at[i, at(tx * 8, 8), CB], r2.at[i, s - 1, :, CB], at_x(s)
            elif k == 2:
                a = q2.at[i, mine_a, CA], q2.at[i, mine_a, CA], at_z(s)
                b = q2.at[i, mine_b, CB], q2.at[i, mine_b, CB], at_x(s)
            else:
                a = q2.at[i, at(x * 32, 32), CA], q2.at[i, at(x * 32, 32), CA], at_x(s)
                b = q2.at[i, at(z * 32, 32), CB], q2.at[i, at(z * 32, 32), CB], at_z(s)
            for h, (src, dst, to) in enumerate((a, b)):
                out.append(pltpu.make_async_remote_copy(
                    src_ref=src, dst_ref=dst, send_sem=g_ss.at[i, k, h, s - 1], recv_sem=g_rs.at[i, k, h, s - 1],
                    device_id=to, device_id_type=MESH,
                ))
        return out

    def begin(i, k):
        for copy in stage(i, k):
            copy.start()

    def after(i, k):
        for copy in stage(i, k):
            copy.wait()
        if k == 0:
            q1[i, :, CA] = (pack[i, at(x * 32, 32), CA] + r1[i, 0, :, CA]) + (r1[i, 1, :, CA] + r1[i, 2, :, CA])
            q1[i, :, CB] = (pack[i, at(z * 32, 32), CB] + r1[i, 0, :, CB]) + (r1[i, 1, :, CB] + r1[i, 2, :, CB])
        elif k == 1:
            q2[i, mine_a, CA] = (q1[i, at(z * 8, 8), CA] + r2[i, 0, :, CA]) + (r2[i, 1, :, CA] + r2[i, 2, :, CA])
            q2[i, mine_b, CB] = (q1[i, at(x * 8, 8), CB] + r2[i, 0, :, CB]) + (r2[i, 1, :, CB] + r2[i, 2, :, CB])
        if k < 3:
            begin(i, k + 1)
            return
        same = lax.broadcasted_iota(jnp.int32, (128, 128), 0) == lax.broadcasted_iota(jnp.int32, (128, 128), 1)
        for b in (i, 5 - i):
            y0, w = b * 128, width - 128 * b
            lead = 0 if b < 3 else width + 128 - w
            A[y0:y0 + 128, y0:y0 + 128] += q2[i, :, lead:lead + 128] + jnp.where(same, damping, 0.0)
            if w > 128:
                A[y0:y0 + 128, y0 + 128:] += q2[i, :, lead + 128:lead + w]

    fill(0)
    begin(0, 0)
    fill(1)
    begin(1, 0)
    fill(2)
    after(0, 0)
    begin(2, 0)
    after(0, 1)
    after(1, 0)
    after(0, 2)
    after(1, 1)
    after(2, 0)
    after(1, 2)
    after(0, 3)

    def body(kb, _):
        row = pl.multiple_of(kb * 128, 128)
        for q in (1, 2):
            @pl.when(kb == q)
            def _():
                after(q, 3)

        blk = A[pl.ds(row, 128), pl.ds(row, 128)]
        up, lo = factor8([blk[8 * t:8 * t + 8] for t in range(16)])

        @pl.when(kb == 0)
        def _():
            after(2, 1)

        for t in range(16):
            R[pl.ds(row + 8 * t, 8), pl.ds(row, 128)] = up[t]
            L[8 * t:8 * t + 8, :] = lo[t]
        for q in range(5):
            @pl.when(kb == q)
            def _():
                x0 = (q + 1) * 128
                panel = jnp.dot(L[...], A[q * 128:x0, x0:], precision=HI, preferred_element_type=jnp.float32)
                R[q * 128:x0, x0:] = panel
                if q == 0:
                    after(2, 2)
                for i in range(q + 1, 6):
                    y0 = i * 128
                    A[y0:y0 + 128, y0:] -= lax.dot_general(
                        panel[:, y0 - x0:y0 - x0 + 128], panel[:, y0 - x0:], (((0,), (0,)), ((), ())), precision=HI,
                        preferred_element_type=jnp.float32,
                    )
        return 0

    lax.fori_loop(0, 6, body, 0)
    r_ref[...] = R[at(d * 48, 48), :]
    own_d.wait()
    for i in range(6):
        y0 = i * 128
        p_ref[y0:y0 + 128, :] = jnp.dot(
            R[y0:y0 + 128, y0:], down[y0:, :].astype(jnp.float32), precision=HI, preferred_element_type=jnp.float32
        )


def lanes(v, k):
    return jnp.take_along_axis(v, jnp.full((8,128), k, jnp.int32), axis=1)
def subl(v, r):
    return jnp.broadcast_to(v[r:r+1, :], (8, 128))

def factor8(M):
    M = list(M)
    lane = lax.broadcasted_iota(jnp.int32, (8,128), 1)
    sub = lax.broadcasted_iota(jnp.int32, (8,128), 0)
    up, lo = [], []
    for q in range(16):
        k0 = 8*q
        C = {t: [lanes(M[t], k0+j) for j in range(8)] for t in range(q, 16)}
        E = list(C[q])
        own = (lane >= k0) & (lane < k0+8)
        ident = (lane == sub + k0).astype(jnp.float32)
        V = M[q]
        N = jnp.where(own, ident, M[q])
        F = N
        U = V
        dinv = jnp.zeros((8,128), jnp.float32)
        for j in range(8):
            d = subl(E[j], j)
            inv = 1.0 / d
            dinv = jnp.where(sub == j, inv, dinv)
            s = E[j] * inv
            fj = jnp.where(sub == j, 1.0 - inv, s)
            ff = jnp.where(sub > j, s, 0.0)
            for i in range(j+1, 8):
                E[i] = E[i] - fj * subl(E[i], j)
            N, F, U = N - fj * subl(N, j), F - ff * subl(F, j), U - ff * subl(U, j)
        rs = jnp.sqrt(dinv)
        U, F = U*rs, F*rs
        up.append(jnp.where(lane >= sub + k0, U, 0.0))
        lo.append(jnp.where(lane <= sub + k0, F, 0.0))
        G = [subl(N, j) for j in range(8)]
        for t in range(q+1, 16):
            base = jnp.where(own, 0.0, M[t])
            c = C[t]
            a = (c[0]*G[0] + c[1]*G[1]) + (c[2]*G[2] + c[3]*G[3])
            b = (c[4]*G[4] + c[5]*G[5]) + (c[6]*G[6] + c[7]*G[7])
            M[t] = base - (a + b)
    return up, lo

def factors(tokens, ids, gate, up, down, rows_avg):
    model, width = tokens.shape[1], gate.shape[1]
    any_, vmem = pl.BlockSpec(memory_space=pl.ANY), pl.BlockSpec(memory_space=pltpu.VMEM)
    bf, f32, dma = jnp.bfloat16, jnp.float32, pltpu.SemaphoreType.DMA
    return pl.pallas_call(
        functools.partial(whole_kernel, float(rows_avg)),
        out_shape=(jax.ShapeDtypeStruct((width // 16, width), f32), jax.ShapeDtypeStruct(down.shape, f32)),
        in_specs=[any_, pl.BlockSpec(memory_space=pltpu.SMEM), any_, any_, any_],
        out_specs=(vmem, vmem),
        scratch_shapes=[
            pltpu.VMEM((9, BROWS, model), bf),
            pltpu.VMEM((8, 2, BROWS, model), bf),
            pltpu.VMEM((8, 2, BROWS, model), bf),
            pltpu.VMEM((4, 4, model // 16, width), bf),
            pltpu.VMEM((4, 4, model // 16, width), bf),
            pltpu.VMEM((4 * PAIR, width), bf),
            pltpu.VMEM((width, width), f32),
            pltpu.VMEM((3, 128, width + 128), f32),
            pltpu.VMEM((3, 3, 32, width + 128), f32),
            pltpu.VMEM((3, 32, width + 128), f32),
            pltpu.VMEM((3, 3, 8, width + 128), f32),
            pltpu.VMEM((3, 128, width + 128), f32),
            pltpu.VMEM(down.shape, bf),
            pltpu.VMEM((width, width), f32),
            pltpu.VMEM((width, width), f32),
            pltpu.VMEM((128, 128), f32),
            dma((4,)), dma((8, 2)), dma((8, 2)), dma((4, 3)), dma((4, 3)), dma((3, 4, 2, 3)), dma((3, 4, 2, 3)),
        ],
        compiler_params=pltpu.CompilerParams(collective_id=1, has_side_effects=True, vmem_limit_bytes=58 << 20),
    )(tokens.reshape(8, BROWS, model), ids, gate, up, down)


def on_device(tokens, block_expert, gate_weight, up_weight, down_weight):
    rows_avg = tokens.shape[0] * lax.axis_size("expert") * lax.axis_size("dp") // lax.axis_size("expert")
    factor, product = factors(tokens, block_expert[:, 0], gate_weight[0], up_weight[0], down_weight[0], rows_avg)
    return (factor[None], product[None])


def solution(mesh):
    placed = (
        P(("expert", "dp"), None),
        P(("expert", "dp"), None),
        P("expert", "dp", None),
        P("expert", "dp", None),
        P("expert", None, "dp"),
    )
    return jax.shard_map(
        on_device,
        mesh=mesh,
        in_specs=placed,
        out_specs=(P("expert", "dp", None), P("expert", None, "dp")),
        check_vma=False,
    )
```

```python
import functools

import jax
import jax.numpy as jnp
from jax import lax
from jax.experimental import pallas as pl
from jax.experimental.pallas import tpu as pltpu
from jax.sharding import PartitionSpec as P

BROWS = 128
HI = lax.Precision.HIGHEST
damping = 0.05
MESH = pl.DeviceIdType.MESH
PAIR = 2 * BROWS
NEAR = ((0, 1, 0, 1, 0), (0, 1, 1, 1, 1))
STEPS = (
    ((2, 0, 0, 2, 0),),
    ((2, 0, 1, 2, 1),),
    ((2, 1, 0, 3, 0),),
    ((2, 1, 1, 3, 1),),
    ((1, 0, 0, 4, 0), (3, 0, 0, 4, 1)),
    ((1, 0, 1, 5, 0), (3, 0, 1, 5, 1)),
    ((1, 1, 0, 6, 0), (3, 1, 0, 6, 1)),
    ((1, 1, 1, 7, 0), (3, 1, 1, 7, 1)),
)
AHEAD = 3


def whole_kernel(rows_avg, tok_ref, ids_ref, gate_ref, up_ref, down_ref, r_ref, p_ref,
                  tok, send, got, wg, wu, hid, acc, pack, r1, q1, r2, q2, down, A, R, L,
                  local_sem, tok_ss, tok_rs, w_ss, w_rs, g_ss, g_rs):
    e, d = lax.axis_index("expert"), lax.axis_index("dp")
    y, c, x, z = e // 2, e % 2, d // 4, d % 4

    def at_y(dy, dc):
        return {"expert": ((y + dy) % 4) * 2 + (c + dc) % 2, "dp": d}

    def at_x(s):
        return {"expert": e, "dp": ((x + s) % 4) * 4 + z}

    def at_z(s):
        return {"expert": e, "dp": x * 4 + (z + s) % 4}

    bar = pltpu.get_barrier_semaphore()
    for dy, dc in ((0, 1), (1, 0), (1, 1), (2, 0), (2, 1), (3, 0), (3, 1)):
        pl.semaphore_signal(bar, inc=1, device_id=at_y(dy, dc), device_id_type=MESH)
    for s in (1, 2, 3):
        pl.semaphore_signal(bar, inc=1, device_id=at_x(s), device_id_type=MESH)
        pl.semaphore_signal(bar, inc=1, device_id=at_z(s), device_id_type=MESH)
    load = pltpu.make_async_copy(tok_ref, tok.at[pl.ds(0, 8)], local_sem.at[0])
    load.start()
    own_g = pltpu.make_async_copy(gate_ref, wg.at[x, z], local_sem.at[1])
    own_u = pltpu.make_async_copy(up_ref, wu.at[x, z], local_sem.at[2])
    own_d = pltpu.make_async_copy(down_ref, down, local_sem.at[3])
    own_d.start()
    own_g.start()
    own_u.start()
    pl.semaphore_wait(bar, 13)

    def remote(src, dst, ss, rs, to):
        copy = pltpu.make_async_remote_copy(src_ref=src, dst_ref=dst, send_sem=ss, recv_sem=rs, device_id=to, device_id_type=MESH)
        copy.start()
        return copy

    first = []
    for s in (1, 2, 3):
        first.append(remote(gate_ref, wg.at[x, z], w_ss.at[0, s - 1], w_rs.at[0, s - 1], at_x(s)))
        first.append(remote(up_ref, wu.at[x, z], w_ss.at[1, s - 1], w_rs.at[1, s - 1], at_z(s)))

    ids = [ids_ref[b] for b in range(8)]

    def slot(dy, dc, second):
        want = ((y + dy) % 4) * 2 + (c + dc) % 2
        one = two = jnp.int32(8)
        for b in range(7, -1, -1):
            hit = ids[b] == want
            two = jnp.where(hit, one, two)
            one = jnp.where(hit, jnp.int32(b), one)
        return two if second else one

    tok[8] = jnp.zeros_like(tok[8])
    load.wait()

    def block_copy(dy, dc, second, u, half):
        return pltpu.make_async_remote_copy(
            src_ref=send.at[u, half], dst_ref=got.at[u, half], send_sem=tok_ss.at[u, half], recv_sem=tok_rs.at[u, half],
            device_id=at_y(dy, dc), device_id_type=MESH,
        )

    def post(blocks):
        for b in blocks:
            send[b[3], b[4]] = tok[slot(*b[:3])]
            block_copy(*b).start()

    def sent(blocks):
        for b in blocks:
            block_copy(*b).wait_send()

    for n in range(AHEAD):
        post(STEPS[n])
    post(NEAR)
    for k in range(2):
        got[0, k] = tok[slot(0, 0, k)]
    acc[...] = jnp.zeros_like(acc)
    A[...] = jnp.zeros_like(A)
    R[...] = jnp.zeros_like(R)

    own_g.wait()
    own_u.wait()
    for copy in first:
        copy.wait()
    second = []
    for s in (1, 2, 3):
        second.append(remote(wg.at[:, z], wg.at[:, z], w_ss.at[2, s - 1], w_rs.at[2, s - 1], at_z(s)))
        second.append(remote(wu.at[x], wu.at[x], w_ss.at[3, s - 1], w_rs.at[3, s - 1], at_x(s)))
    for n in range(AHEAD, 6):
        sent(STEPS[n - AHEAD])
        post(STEPS[n])
    sent(NEAR)
    for copy in second:
        copy.wait()

    model, width = 16 * wg.shape[2], wg.shape[3]

    def unit(u, _):
        for n in (6, 7):
            @pl.when(u == n - 3)
            def _():
                sent(STEPS[n - AHEAD])
                post(STEPS[n])

        for blocks in (NEAR, STEPS[0] + STEPS[1], STEPS[2] + STEPS[3]) + STEPS[4:]:
            @pl.when(u == blocks[0][3])
            def _():
                for b in blocks:
                    block_copy(*b).wait_recv()

        def part(n, _):
            cut = pl.ds(pl.multiple_of(n * 256, 256), 256)
            rows = got[u].reshape(PAIR, model)
            gate = jnp.dot(rows, wg[:, :, :, cut].reshape(model, 256), preferred_element_type=jnp.float32)
            lifted = jnp.dot(rows, wu[:, :, :, cut].reshape(model, 256), preferred_element_type=jnp.float32)
            hidden = gate / (1.0 + jnp.exp(-gate)) * lifted
            high = hidden.astype(jnp.bfloat16)
            low = (hidden - high.astype(jnp.float32)).astype(jnp.bfloat16)
            hid[0:256, cut] = high
            hid[256:512, cut] = high
            hid[512:768, cut] = low
            hid[768:1024, cut] = high
            return 0

        lax.fori_loop(0, width // 256, part, 0)
        for i in range(0, width, 256):
            acc[i:i + 256, i:] += lax.dot_general(
                hid[0:768, i:i + 256], hid[256:1024, i:], (((0,), (0,)), ((), ())), preferred_element_type=jnp.float32
            )
        return 0

    lax.fori_loop(0, 8, unit, 0)
    for n in range(8 - AHEAD, 8):
        sent(STEPS[n])

    def fill(i):
        w = width - 128 * i
        top, low = i * 128, (5 - i) * 128
        pack[i, :, 0:w] = acc[top:top + 128, top:] * (1.0 / rows_avg)
        pack[i, :, w:] = acc[low:low + 128, low:] * (1.0 / rows_avg)

    CA, CB = pl.ds(0, 512), pl.ds(512, 384)

    def at(r, n):
        return pl.ds(pl.multiple_of(r, 8), n)

    mine_a, mine_b = at(x * 32 + z * 8, 8), at(z * 32 + x * 8, 8)

    def stage(i, k):
        out = []
        for s in (1, 2, 3):
            tx, tz = (x + s) % 4, (z + s) % 4
            if k == 0:
                a = pack.at[i, at(tx * 32, 32), CA], r1.at[i, s - 1, :, CA], at_x(s)
                b = pack.at[i, at(tz * 32, 32), CB], r1.at[i, s - 1, :, CB], at_z(s)
            elif k == 1:
                a = q1.at[i, at(tz * 8, 8), CA], r2.at[i, s - 1, :, CA], at_z(s)
                b = q1.at[i, at(tx * 8, 8), CB], r2.at[i, s - 1, :, CB], at_x(s)
            elif k == 2:
                a = q2.at[i, mine_a, CA], q2.at[i, mine_a, CA], at_z(s)
                b = q2.at[i, mine_b, CB], q2.at[i, mine_b, CB], at_x(s)
            else:
                a = q2.at[i, at(x * 32, 32), CA], q2.at[i, at(x * 32, 32), CA], at_x(s)
                b = q2.at[i, at(z * 32, 32), CB], q2.at[i, at(z * 32, 32), CB], at_z(s)
            for h, (src, dst, to) in enumerate((a, b)):
                out.append(pltpu.make_async_remote_copy(
                    src_ref=src, dst_ref=dst, send_sem=g_ss.at[i, k, h, s - 1], recv_sem=g_rs.at[i, k, h, s - 1],
                    device_id=to, device_id_type=MESH,
                ))
        return out

    def begin(i, k):
        for copy in stage(i, k):
            copy.start()

    def after(i, k):
        for copy in stage(i, k):
            copy.wait()
        if k == 0:
            q1[i, :, CA] = (pack[i, at(x * 32, 32), CA] + r1[i, 0, :, CA]) + (r1[i, 1, :, CA] + r1[i, 2, :, CA])
            q1[i, :, CB] = (pack[i, at(z * 32, 32), CB] + r1[i, 0, :, CB]) + (r1[i, 1, :, CB] + r1[i, 2, :, CB])
        elif k == 1:
            q2[i, mine_a, CA] = (q1[i, at(z * 8, 8), CA] + r2[i, 0, :, CA]) + (r2[i, 1, :, CA] + r2[i, 2, :, CA])
            q2[i, mine_b, CB] = (q1[i, at(x * 8, 8), CB] + r2[i, 0, :, CB]) + (r2[i, 1, :, CB] + r2[i, 2, :, CB])
        if k < 3:
            begin(i, k + 1)
            return
        same = lax.broadcasted_iota(jnp.int32, (128, 128), 0) == lax.broadcasted_iota(jnp.int32, (128, 128), 1)
        for b in (i, 5 - i):
            y0, w = b * 128, width - 128 * b
            lead = 0 if b < 3 else width + 128 - w
            A[y0:y0 + 128, y0:y0 + 128] += q2[i, :, lead:lead + 128] + jnp.where(same, damping, 0.0)
            if w > 128:
                A[y0:y0 + 128, y0 + 128:] += q2[i, :, lead + 128:lead + w]

    fill(0)
    begin(0, 0)
    fill(1)
    begin(1, 0)
    fill(2)
    after(0, 0)
    begin(2, 0)
    after(0, 1)
    after(1, 0)
    after(0, 2)
    after(1, 1)
    after(2, 0)
    after(1, 2)
    after(0, 3)

    def body(kb, _):
        row = pl.multiple_of(kb * 128, 128)
        for q in (1, 2):
            @pl.when(kb == q)
            def _():
                after(q, 3)

        blk = A[pl.ds(row, 128), pl.ds(row, 128)]
        up, lo = factor([blk[8 * t:8 * t + 8] for t in range(16)], 16)

        @pl.when(kb == 0)
        def _():
            after(2, 1)

        for t in range(16):
            R[pl.ds(row + 8 * t, 8), pl.ds(row, 128)] = up[t]
            L[8 * t:8 * t + 8, :] = lo[t]
        for q in range(5):
            @pl.when(kb == q)
            def _():
                x0 = (q + 1) * 128
                panel = jnp.dot(L[...], A[q * 128:x0, x0:], precision=HI, preferred_element_type=jnp.float32)
                R[q * 128:x0, x0:] = panel
                if q == 0:
                    after(2, 2)
                for i in range(q + 1, 6):
                    y0 = i * 128
                    A[y0:y0 + 128, y0:] -= lax.dot_general(
                        panel[:, y0 - x0:y0 - x0 + 128], panel[:, y0 - x0:], (((0,), (0,)), ((), ())), precision=HI,
                        preferred_element_type=jnp.float32,
                    )
        return 0

    lax.fori_loop(0, 6, body, 0)
    r_ref[...] = R[at(d * 48, 48), :]
    own_d.wait()
    for i in range(6):
        y0 = i * 128
        p_ref[y0:y0 + 128, :] = jnp.dot(
            R[y0:y0 + 128, y0:], down[y0:, :].astype(jnp.float32), precision=HI, preferred_element_type=jnp.float32
        )


def lanes(v, k):
    return jnp.take_along_axis(v, jnp.full((8, 128), k, jnp.int32), axis=1)


def subl(v, r):
    return jnp.broadcast_to(v[r:r + 1, :], (8, 128))


def factor(M, wide):
    M, tall = list(M), wide // 8
    lane = lax.broadcasted_iota(jnp.int32, (8, 128), 1)
    sub = lax.broadcasted_iota(jnp.int32, (8, 128), 0)
    zero = jnp.zeros((8, 128), jnp.float32)
    up, lo = [], []
    for q in range(0, 16, tall):
        k0 = 8 * q
        C = {t: [lanes(M[t], k0 + j) for j in range(wide)] for t in range(q, 16)}
        E = [[C[q + h][j] for h in range(tall)] for j in range(wide)]
        own = (lane >= k0) & (lane < k0 + wide)
        U = [M[q + h] for h in range(tall)]
        N = [jnp.where(own, (lane == sub + (k0 + 8 * h)).astype(jnp.float32), U[h]) for h in range(tall)]
        F = list(N)
        scale = [zero] * tall
        for j in range(0, wide, 2):
            g, r = divmod(j, 8)
            a, b, e = subl(E[j][g], r), subl(E[j + 1][g], r), subl(E[j + 1][g], r + 1)
            inv = 1.0 / (a * e - b * b)
            ia = 1.0 / a
            scale[g] = jnp.where(sub == r, ia, jnp.where(sub == r + 1, a * inv, scale[g]))
            ai, bi, ei = a * inv, b * inv, e * inv
            f0, f1, w0, w1 = [], [], [], []
            for h in range(tall):
                x0 = E[j][h] * ei - E[j + 1][h] * bi
                x1 = E[j + 1][h] * ai - E[j][h] * bi
                w0.append(x0 if h > g else jnp.where(sub > r + 1, x0, jnp.where(sub == r + 1, b * ia, 0.0)) if h == g else None)
                w1.append(x1 if h > g else jnp.where(sub > r + 1, x1, 0.0) if h == g else None)
                if h == g:
                    x0 = jnp.where(sub == r, -ei, jnp.where(sub == r + 1, bi, x0))
                    x1 = jnp.where(sub == r, bi, jnp.where(sub == r + 1, -ai, x1))
                f0.append(x0)
                f1.append(x1)
            pair = (sub == r) | (sub == r + 1)

            def jordan(V):
                p, s = subl(V[g], r), subl(V[g], r + 1)
                return [(jnp.where(pair, 0.0, V[h]) if h == g else V[h]) - (f0[h] * p + f1[h] * s) for h in range(tall)]

            def forward(V):
                p, s = subl(V[g], r), subl(V[g], r + 1)
                return [V[h] if h < g else V[h] - (w0[h] * p + w1[h] * s) for h in range(tall)]

            for i in range(j + 2, wide):
                E[i] = jordan(E[i])
            N, F, U = jordan(N), forward(F), forward(U)
        for h in range(tall):
            root = jnp.sqrt(scale[h])
            up.append(jnp.where(lane >= sub + (k0 + 8 * h), U[h] * root, 0.0))
            lo.append(jnp.where(lane <= sub + (k0 + 8 * h), F[h] * root, 0.0))
        G = [subl(N[j // 8], j % 8) for j in range(wide)]
        for t in range(q + tall, 16):
            terms = [C[t][j] * G[j] for j in range(wide)]
            while len(terms) > 1:
                terms = [terms[i] + terms[i + 1] for i in range(0, len(terms), 2)]
            M[t] = jnp.where(own, 0.0, M[t]) - terms[0]
    return up, lo


def factors(tokens, ids, gate, up, down, rows_avg):
    model, width = tokens.shape[1], gate.shape[1]
    any_, vmem = pl.BlockSpec(memory_space=pl.ANY), pl.BlockSpec(memory_space=pltpu.VMEM)
    bf, f32, dma = jnp.bfloat16, jnp.float32, pltpu.SemaphoreType.DMA
    return pl.pallas_call(
        functools.partial(whole_kernel, float(rows_avg)),
        out_shape=(jax.ShapeDtypeStruct((width // 16, width), f32), jax.ShapeDtypeStruct(down.shape, f32)),
        in_specs=[any_, pl.BlockSpec(memory_space=pltpu.SMEM), any_, any_, any_],
        out_specs=(vmem, vmem),
        scratch_shapes=[
            pltpu.VMEM((9, BROWS, model), bf),
            pltpu.VMEM((8, 2, BROWS, model), bf),
            pltpu.VMEM((8, 2, BROWS, model), bf),
            pltpu.VMEM((4, 4, model // 16, width), bf),
            pltpu.VMEM((4, 4, model // 16, width), bf),
            pltpu.VMEM((4 * PAIR, width), bf),
            pltpu.VMEM((width, width), f32),
            pltpu.VMEM((3, 128, width + 128), f32),
            pltpu.VMEM((3, 3, 32, width + 128), f32),
            pltpu.VMEM((3, 32, width + 128), f32),
            pltpu.VMEM((3, 3, 8, width + 128), f32),
            pltpu.VMEM((3, 128, width + 128), f32),
            pltpu.VMEM(down.shape, bf),
            pltpu.VMEM((width, width), f32),
            pltpu.VMEM((width, width), f32),
            pltpu.VMEM((128, 128), f32),
            dma((4,)), dma((8, 2)), dma((8, 2)), dma((4, 3)), dma((4, 3)), dma((3, 4, 2, 3)), dma((3, 4, 2, 3)),
        ],
        compiler_params=pltpu.CompilerParams(collective_id=1, has_side_effects=True, vmem_limit_bytes=58 << 20),
    )(tokens.reshape(8, BROWS, model), ids, gate, up, down)


def on_device(tokens, block_expert, gate_weight, up_weight, down_weight):
    rows_avg = tokens.shape[0] * lax.axis_size("expert") * lax.axis_size("dp") // lax.axis_size("expert")
    factor, product = factors(tokens, block_expert[:, 0], gate_weight[0], up_weight[0], down_weight[0], rows_avg)
    return (factor[None], product[None])


def solution(mesh):
    placed = (
        P(("expert", "dp"), None),
        P(("expert", "dp"), None),
        P("expert", "dp", None),
        P("expert", "dp", None),
        P("expert", None, "dp"),
    )
    return jax.shard_map(
        on_device,
        mesh=mesh,
        in_specs=placed,
        out_specs=(P("expert", "dp", None), P("expert", None, "dp")),
        check_vma=False,
    )
```

```python
import functools

import jax
import jax.numpy as jnp
from jax import lax
from jax.experimental import pallas as pl
from jax.experimental.pallas import tpu as pltpu
from jax.sharding import PartitionSpec as P

BROWS = 128
HI = lax.Precision.HIGHEST
damping = 0.05
MESH = pl.DeviceIdType.MESH
PAIR = 2 * BROWS
STEPS = (
    ((2, 1, 0, 2, 2),),
    ((2, 1, 1, 2, 3),),
    ((2, 0, 0, 1, 4), (3, 1, 0, 3, 4)),
    ((2, 0, 1, 1, 5), (3, 1, 1, 3, 5)),
    ((1, 1, 0, 1, 6), (3, 0, 0, 3, 6)),
    ((1, 1, 1, 1, 7), (3, 0, 1, 3, 7)),
)
AHEAD = 3


def whole_kernel(rows_avg, tok_ref, ids_ref, gate_ref, up_ref, down_ref, r_ref, p_ref,
                 tok, send, near, got, wg, wu, hid, acc, pack, r1, q1, r2, q2, bq, bs, down, A, R, L,
                 local_sem, tok_ss, near_ss, tok_rs, w_ss, w_rs, h_ss, h_rs, g_ss, g_rs):
    e, d = lax.axis_index("expert"), lax.axis_index("dp")
    y, c, x, z = e // 2, e % 2, d // 4, d % 4
    sibling = {"expert": y * 2 + 1 - c, "dp": d}

    def at_y(dy, core):
        return {"expert": ((y + dy) % 4) * 2 + core, "dp": d}

    def at_x(s):
        return {"expert": e, "dp": ((x + s) % 4) * 4 + z}

    def at_z(s):
        return {"expert": e, "dp": x * 4 + (z + s) % 4}

    bar = pltpu.get_barrier_semaphore()
    pl.semaphore_signal(bar, inc=1, device_id=sibling, device_id_type=MESH)
    for dy in (1, 2, 3):
        for core in (0, 1):
            pl.semaphore_signal(bar, inc=1, device_id=at_y(dy, core), device_id_type=MESH)
    for s in (1, 2, 3):
        pl.semaphore_signal(bar, inc=1, device_id=at_x(s), device_id_type=MESH)
        pl.semaphore_signal(bar, inc=1, device_id=at_z(s), device_id_type=MESH)
    load = pltpu.make_async_copy(tok_ref, tok.at[pl.ds(0, 8)], local_sem.at[0])
    load.start()
    own_g = pltpu.make_async_copy(gate_ref, wg.at[0, x, z], local_sem.at[1])
    own_u = pltpu.make_async_copy(up_ref, wu.at[0, x, z], local_sem.at[2])
    own_d = pltpu.make_async_copy(down_ref, down, local_sem.at[3])
    own_d.start()
    own_g.start()
    own_u.start()
    pl.semaphore_wait(bar, 13)

    def remote(src, dst, ss, rs, to):
        return pltpu.make_async_remote_copy(src_ref=src, dst_ref=dst, send_sem=ss, recv_sem=rs, device_id=to, device_id_type=MESH)

    def weights(m, k):
        out = []
        for s in (1, 2, 3):
            if k == 0:
                a, b = gate_ref if m == 0 else wg.at[m, x, z], up_ref if m == 0 else wu.at[m, x, z]
                out.append(remote(a, wg.at[m, x, z], w_ss.at[m, 0, 0, s - 1], w_rs.at[m, 0, 0, s - 1], at_x(s)))
                out.append(remote(b, wu.at[m, x, z], w_ss.at[m, 0, 1, s - 1], w_rs.at[m, 0, 1, s - 1], at_z(s)))
            elif k == 1 and s != 2:
                out.append(remote(wg.at[m, :, z], wg.at[m, :, z], w_ss.at[m, 1, 0, s - 1], w_rs.at[m, 1, 0, s - 1], at_z(s)))
                out.append(remote(wu.at[m, x], wu.at[m, x], w_ss.at[m, 1, 1, s - 1], w_rs.at[m, 1, 1, s - 1], at_x(s)))
            elif k == 2 and s != 2:
                half, fz, fx = pl.ds(s - 1, 2), (z + 4 - s) % 4, (x + 4 - s) % 4
                a, b = wg.at[m, half, fz], wu.at[m, fx, half]
                out.append(remote(a, a, w_ss.at[m, 2, 0, s - 1], w_rs.at[m, 2, 0, s - 1], at_z(s)))
                out.append(remote(b, b, w_ss.at[m, 2, 1, s - 1], w_rs.at[m, 2, 1, s - 1], at_x(s)))
        return out

    def shard():
        return [
            remote(gate_ref, wg.at[1, x, z], h_ss.at[0], h_rs.at[0], at_y(3, 0)),
            remote(up_ref, wu.at[1, x, z], h_ss.at[1], h_rs.at[1], at_y(3, 0)),
        ]

    def start(copies):
        for copy in copies:
            copy.start()

    def wait(copies):
        for copy in copies:
            copy.wait()

    start(weights(0, 0))

    @pl.when(c == 0)
    def _():
        start(shard())

    ids = [ids_ref[b] for b in range(8)]

    def slot(dy, core, second):
        want = ((y + dy) % 4) * 2 + core
        one = two = jnp.int32(8)
        for b in range(7, -1, -1):
            hit = ids[b] == want
            two = jnp.where(hit, one, two)
            one = jnp.where(hit, jnp.int32(b), one)
        return two if second else one

    tok[8] = jnp.zeros_like(tok[8])
    load.wait()

    def block_copy(n, k):
        dy, core, _, to, u = STEPS[n][k]
        return remote(send.at[n, k], got.at[u, c], tok_ss.at[n, k], tok_rs.at[u, c], at_y(to, core))

    def post(n):
        for k, b in enumerate(STEPS[n]):
            send[n, k] = tok[slot(*b[:3])]
            block_copy(n, k).start()

    def sent(n):
        for k in range(len(STEPS[n])):
            block_copy(n, k).wait_send()

    def near_copy(u, k):
        return remote(near.at[u // 2, k], got.at[u, k], near_ss.at[u // 2, k], tok_rs.at[u, k], sibling)

    for n in range(AHEAD):
        post(n)
    for k in range(2):
        near[0, k] = tok[slot(0, 1 - c, k)]
        near_copy(1, k).start()
        got[0, k] = tok[slot(0, c, k)]

    @pl.when(c == 0)
    def _():
        for k in range(2):
            got[2, k] = tok[slot(1, 0, k)]

    @pl.when(c == 1)
    def _():
        for k in range(2):
            near[1, k] = tok[slot(1, 0, k)]
            near_copy(3, k).start()

    acc[...] = jnp.zeros_like(acc)
    A[...] = jnp.zeros_like(A)
    R[...] = jnp.zeros_like(R)

    own_g.wait()
    own_u.wait()
    wait(weights(0, 0))
    start(weights(0, 1))

    @pl.when(c == 0)
    def _():
        wait(shard())
        start(weights(1, 0))

    wait(weights(0, 1))
    start(weights(0, 2))

    @pl.when(c == 0)
    def _():
        wait(weights(1, 0))
        start(weights(1, 1))

    for n in range(AHEAD, len(STEPS)):
        sent(n - AHEAD)
        post(n)
    for k in range(2):
        near_copy(1, k).wait_send()

    @pl.when(c == 1)
    def _():
        for k in range(2):
            near_copy(3, k).wait_send()

    wait(weights(0, 2))
    model, width = 16 * wg.shape[3], wg.shape[4]

    def landed(u):
        for k in range(2):
            remote(near.at[0, k], got.at[u, k], near_ss.at[0, k], tok_rs.at[u, k], sibling).wait_recv()

    CA, CB = pl.ds(0, 512), pl.ds(512, 384)

    def at(r, n):
        return pl.ds(pl.multiple_of(r, 8), n)

    mine_a, mine_b = at(x * 32 + z * 8, 8), at(z * 32 + x * 8, 8)

    def fill(m, i):
        w = width - 128 * i
        top, low = i * 128, (5 - i) * 128
        pack[m, i, :, 0:w] = acc[m, top:top + 128, top:] * (1.0 / rows_avg)
        pack[m, i, :, w:] = acc[m, low:low + 128, low:] * (1.0 / rows_avg)

    def stage(m, i, k):
        out = []
        for s in (1, 2, 3):
            tx, tz = (x + s) % 4, (z + s) % 4
            if k == 0:
                a = pack.at[m, i, at(tx * 32, 32), CA], r1.at[m, i, s - 1, :, CA], at_x(s)
                b = pack.at[m, i, at(tz * 32, 32), CB], r1.at[m, i, s - 1, :, CB], at_z(s)
            elif k == 1:
                a = q1.at[m, i, at(tz * 8, 8), CA], r2.at[m, i, s - 1, :, CA], at_z(s)
                b = q1.at[m, i, at(tx * 8, 8), CB], r2.at[m, i, s - 1, :, CB], at_x(s)
            elif k == 2:
                a = q2.at[i, mine_a, CA], q2.at[i, mine_a, CA], at_z(s)
                b = q2.at[i, mine_b, CB], q2.at[i, mine_b, CB], at_x(s)
            else:
                a = q2.at[i, at(x * 32, 32), CA], q2.at[i, at(x * 32, 32), CA], at_x(s)
                b = q2.at[i, at(z * 32, 32), CB], q2.at[i, at(z * 32, 32), CB], at_z(s)
            for h, (src, dst, to) in enumerate((a, b)):
                out.append(remote(src, dst, g_ss.at[m, i, k, h, s - 1], g_rs.at[m, i, k, h, s - 1], to))
        return out

    def hop():
        return remote(bq, bs, h_ss.at[2], h_rs.at[2], at_y(1, 0))

    def begin(m, i, k):
        start(stage(m, i, k))

    def after(m, i, k):
        wait(stage(m, i, k))
        if k == 0:
            q1[m, i, :, CA] = (pack[m, i, at(x * 32, 32), CA] + r1[m, i, 0, :, CA]) + (r1[m, i, 1, :, CA] + r1[m, i, 2, :, CA])
            q1[m, i, :, CB] = (pack[m, i, at(z * 32, 32), CB] + r1[m, i, 0, :, CB]) + (r1[m, i, 1, :, CB] + r1[m, i, 2, :, CB])
        elif k == 1:
            a = (q1[m, i, at(z * 8, 8), CA] + r2[m, i, 0, :, CA]) + (r2[m, i, 1, :, CA] + r2[m, i, 2, :, CA])
            b = (q1[m, i, at(x * 8, 8), CB] + r2[m, i, 0, :, CB]) + (r2[m, i, 1, :, CB] + r2[m, i, 2, :, CB])
            if m == 1:
                bq[i, :, CA] = a
                bq[i, :, CB] = b
                return
            q2[i, mine_a, CA] = a
            q2[i, mine_b, CB] = b

            @pl.when(c == 0)
            def _():
                q2[i, mine_a, CA] += bs[i, :, CA]
                q2[i, mine_b, CB] += bs[i, :, CB]
        if k < 3:
            begin(m, i, k + 1)
            return
        same = lax.broadcasted_iota(jnp.int32, (128, 128), 0) == lax.broadcasted_iota(jnp.int32, (128, 128), 1)
        for b in (i, 5 - i):
            y0, w = b * 128, width - 128 * b
            lead = 0 if b < 3 else width + 128 - w
            A[y0:y0 + 128, y0:y0 + 128] += q2[i, :, lead:lead + 128] + jnp.where(same, damping, 0.0)
            if w > 128:
                A[y0:y0 + 128, y0 + 128:] += q2[i, :, lead + 128:lead + w]

    def unit(u, _):
        which = (1 - c) * (((u + 2) // 4) % 2)

        @pl.when((c == 0) & (u == 1))
        def _():
            wait(weights(1, 1))
            start(weights(1, 2))

        @pl.when((c == 0) & (u == 2))
        def _():
            wait(weights(1, 2))

        @pl.when((c == 0) & (u == 6))
        def _():
            for i in range(3):
                fill(1, i)
                begin(1, i, 0)

        @pl.when((c == 0) & (u == 7))
        def _():
            for i in range(3):
                after(1, i, 0)

        @pl.when((c == 1) & (u == 2))
        def _():
            landed(2)

        for n in (1, 3, 4, 5, 6, 7):
            @pl.when(u == n)
            def _():
                landed(n)

        def part(n, _):
            cut = pl.ds(pl.multiple_of(n * 256, 256), 256)
            rows = got[u].reshape(PAIR, model)
            gate = jnp.dot(rows, wg[which, :, :, :, cut].reshape(model, 256), preferred_element_type=jnp.float32)
            lifted = jnp.dot(rows, wu[which, :, :, :, cut].reshape(model, 256), preferred_element_type=jnp.float32)
            hidden = gate / (1.0 + jnp.exp(-gate)) * lifted
            high = hidden.astype(jnp.bfloat16)
            low = (hidden - high.astype(jnp.float32)).astype(jnp.bfloat16)
            hid[0:256, cut] = high
            hid[256:512, cut] = high
            hid[512:768, cut] = low
            hid[768:1024, cut] = high
            return 0

        lax.fori_loop(0, width // 256, part, 0)
        for i in range(0, width, 256):
            acc[which, i:i + 256, i:] += lax.dot_general(
                hid[0:768, i:i + 256], hid[256:1024, i:], (((0,), (0,)), ((), ())), preferred_element_type=jnp.float32
            )
        return 0

    lax.fori_loop(0, 8, unit, 0)
    fill(0, 0)
    begin(0, 0, 0)
    fill(0, 1)
    begin(0, 1, 0)

    @pl.when(c == 0)
    def _():
        for i in range(3):
            after(1, i, 1)
        hop().start()

    fill(0, 2)
    for n in range(len(STEPS) - AHEAD, len(STEPS)):
        sent(n)
    after(0, 0, 0)
    begin(0, 2, 0)

    @pl.when(c == 0)
    def _():
        hop().wait()

    after(0, 0, 1)
    after(0, 1, 0)
    after(0, 0, 2)
    after(0, 1, 1)
    after(0, 2, 0)
    after(0, 1, 2)
    after(0, 0, 3)

    def body(kb, _):
        row = pl.multiple_of(kb * 128, 128)
        for q in (1, 2):
            @pl.when(kb == q)
            def _():
                after(0, q, 3)

        blk = A[pl.ds(row, 128), pl.ds(row, 128)]
        up, lo = factor([blk[8 * t:8 * t + 8] for t in range(16)], 16)

        @pl.when(kb == 0)
        def _():
            after(0, 2, 1)

        for t in range(16):
            R[pl.ds(row + 8 * t, 8), pl.ds(row, 128)] = up[t]
            L[8 * t:8 * t + 8, :] = lo[t]
        for q in range(5):
            @pl.when(kb == q)
            def _():
                x0 = (q + 1) * 128
                panel = jnp.dot(L[...], A[q * 128:x0, x0:], precision=HI, preferred_element_type=jnp.float32)
                R[q * 128:x0, x0:] = panel
                if q == 0:
                    after(0, 2, 2)
                for i in range(q + 1, 6):
                    y0 = i * 128
                    A[y0:y0 + 128, y0:] -= lax.dot_general(
                        panel[:, y0 - x0:y0 - x0 + 128], panel[:, y0 - x0:], (((0,), (0,)), ((), ())), precision=HI,
                        preferred_element_type=jnp.float32,
                    )
        return 0

    lax.fori_loop(0, 6, body, 0)
    r_ref[...] = R[at(d * 48, 48), :]
    own_d.wait()
    for i in range(6):
        y0 = i * 128
        p_ref[y0:y0 + 128, :] = jnp.dot(
            R[y0:y0 + 128, y0:], down[y0:, :].astype(jnp.float32), precision=HI, preferred_element_type=jnp.float32
        )


def lanes(v, k):
    return jnp.take_along_axis(v, jnp.full((8, 128), k, jnp.int32), axis=1)


def subl(v, r):
    return jnp.broadcast_to(v[r:r + 1, :], (8, 128))


def factor(M, wide):
    M, tall = list(M), wide // 8
    lane = lax.broadcasted_iota(jnp.int32, (8, 128), 1)
    sub = lax.broadcasted_iota(jnp.int32, (8, 128), 0)
    zero = jnp.zeros((8, 128), jnp.float32)
    up, lo = [], []
    for q in range(0, 16, tall):
        k0 = 8 * q
        C = {t: [lanes(M[t], k0 + j) for j in range(wide)] for t in range(q, 16)}
        E = [[C[q + h][j] for h in range(tall)] for j in range(wide)]
        own = (lane >= k0) & (lane < k0 + wide)
        U = [M[q + h] for h in range(tall)]
        N = [jnp.where(own, (lane == sub + (k0 + 8 * h)).astype(jnp.float32), U[h]) for h in range(tall)]
        F = list(N)
        scale = [zero] * tall
        for j in range(0, wide, 2):
            g, r = divmod(j, 8)
            a, b, e = subl(E[j][g], r), subl(E[j + 1][g], r), subl(E[j + 1][g], r + 1)
            inv = 1.0 / (a * e - b * b)
            ia = 1.0 / a
            scale[g] = jnp.where(sub == r, ia, jnp.where(sub == r + 1, a * inv, scale[g]))
            ai, bi, ei = a * inv, b * inv, e * inv
            f0, f1, w0, w1 = [], [], [], []
            for h in range(tall):
                x0 = E[j][h] * ei - E[j + 1][h] * bi
                x1 = E[j + 1][h] * ai - E[j][h] * bi
                w0.append(x0 if h > g else jnp.where(sub > r + 1, x0, jnp.where(sub == r + 1, b * ia, 0.0)) if h == g else None)
                w1.append(x1 if h > g else jnp.where(sub > r + 1, x1, 0.0) if h == g else None)
                if h == g:
                    x0 = jnp.where(sub == r, -ei, jnp.where(sub == r + 1, bi, x0))
                    x1 = jnp.where(sub == r, bi, jnp.where(sub == r + 1, -ai, x1))
                f0.append(x0)
                f1.append(x1)
            pair = (sub == r) | (sub == r + 1)

            def jordan(V):
                p, s = subl(V[g], r), subl(V[g], r + 1)
                return [(jnp.where(pair, 0.0, V[h]) if h == g else V[h]) - (f0[h] * p + f1[h] * s) for h in range(tall)]

            def forward(V):
                p, s = subl(V[g], r), subl(V[g], r + 1)
                return [V[h] if h < g else V[h] - (w0[h] * p + w1[h] * s) for h in range(tall)]

            for i in range(j + 2, wide):
                E[i] = jordan(E[i])
            N, F, U = jordan(N), forward(F), forward(U)
        for h in range(tall):
            root = jnp.sqrt(scale[h])
            up.append(jnp.where(lane >= sub + (k0 + 8 * h), U[h] * root, 0.0))
            lo.append(jnp.where(lane <= sub + (k0 + 8 * h), F[h] * root, 0.0))
        G = [subl(N[j // 8], j % 8) for j in range(wide)]
        for t in range(q + tall, 16):
            terms = [C[t][j] * G[j] for j in range(wide)]
            while len(terms) > 1:
                terms = [terms[i] + terms[i + 1] for i in range(0, len(terms), 2)]
            M[t] = jnp.where(own, 0.0, M[t]) - terms[0]
    return up, lo


def factors(tokens, ids, gate, up, down, rows_avg):
    model, width = tokens.shape[1], gate.shape[1]
    any_, vmem = pl.BlockSpec(memory_space=pl.ANY), pl.BlockSpec(memory_space=pltpu.VMEM)
    bf, f32, dma = jnp.bfloat16, jnp.float32, pltpu.SemaphoreType.DMA
    return pl.pallas_call(
        functools.partial(whole_kernel, float(rows_avg)),
        out_shape=(jax.ShapeDtypeStruct((width // 16, width), f32), jax.ShapeDtypeStruct(down.shape, f32)),
        in_specs=[any_, pl.BlockSpec(memory_space=pltpu.SMEM), any_, any_, any_],
        out_specs=(vmem, vmem),
        scratch_shapes=[
            pltpu.VMEM((9, BROWS, model), bf),
            pltpu.VMEM((6, 2, BROWS, model), bf),
            pltpu.VMEM((2, 2, BROWS, model), bf),
            pltpu.VMEM((8, 2, BROWS, model), bf),
            pltpu.VMEM((2, 4, 4, model // 16, width), bf),
            pltpu.VMEM((2, 4, 4, model // 16, width), bf),
            pltpu.VMEM((4 * PAIR, width), bf),
            pltpu.VMEM((2, width, width), f32),
            pltpu.VMEM((2, 3, 128, width + 128), f32),
            pltpu.VMEM((2, 3, 3, 32, width + 128), f32),
            pltpu.VMEM((2, 3, 32, width + 128), f32),
            pltpu.VMEM((2, 3, 3, 8, width + 128), f32),
            pltpu.VMEM((3, 128, width + 128), f32),
            pltpu.VMEM((3, 8, width + 128), f32),
            pltpu.VMEM((3, 8, width + 128), f32),
            pltpu.VMEM(down.shape, bf),
            pltpu.VMEM((width, width), f32),
            pltpu.VMEM((width, width), f32),
            pltpu.VMEM((128, 128), f32),
            dma((4,)), dma((6, 2)), dma((2, 2)), dma((8, 2)), dma((2, 3, 2, 3)), dma((2, 3, 2, 3)), dma((3,)), dma((3,)),
            dma((2, 3, 4, 2, 3)), dma((2, 3, 4, 2, 3)),
        ],
        compiler_params=pltpu.CompilerParams(collective_id=1, has_side_effects=True, vmem_limit_bytes=60 << 20),
    )(tokens.reshape(8, BROWS, model), ids, gate, up, down)


def on_device(tokens, block_expert, gate_weight, up_weight, down_weight):
    rows_avg = tokens.shape[0] * lax.axis_size("expert") * lax.axis_size("dp") // lax.axis_size("expert")
    factor, product = factors(tokens, block_expert[:, 0], gate_weight[0], up_weight[0], down_weight[0], rows_avg)
    return (factor[None], product[None])


def solution(mesh):
    placed = (
        P(("expert", "dp"), None),
        P(("expert", "dp"), None),
        P("expert", "dp", None),
        P("expert", "dp", None),
        P("expert", None, "dp"),
    )
    return jax.shard_map(
        on_device,
        mesh=mesh,
        in_specs=placed,
        out_specs=(P("expert", "dp", None), P("expert", None, "dp")),
        check_vma=False,
    )
```

```python
import functools

import jax
import jax.numpy as jnp
from jax import lax
from jax.experimental import pallas as pl
from jax.experimental.pallas import tpu as pltpu
from jax.sharding import PartitionSpec as P

BROWS = 128
HI = lax.Precision.HIGHEST
damping = 0.05
MESH = pl.DeviceIdType.MESH
PAIR = 2 * BROWS
STEPS = (
    ((2, 1, 0, 2, 2),),
    ((2, 1, 1, 2, 3),),
    ((2, 0, 0, 1, 4), (3, 1, 0, 3, 4)),
    ((2, 0, 1, 1, 5), (3, 1, 1, 3, 5)),
    ((1, 1, 0, 1, 6), (3, 0, 0, 3, 6)),
    ((1, 1, 1, 1, 7), (3, 0, 1, 3, 7)),
)
AHEAD = 3


def whole_kernel(rows_avg, tok_ref, ids_ref, gate_ref, up_ref, down_ref, r_ref, p_ref,
                 tok, send, near, got, wg, wu, hid, acc, pack, r1, q1, r2, q2, bq, bs, down, A, R, L,
                 local_sem, tok_ss, near_ss, tok_rs, w_ss, w_rs, h_ss, h_rs, g_ss, g_rs):
    e, d = lax.axis_index("expert"), lax.axis_index("dp")
    y, c, x, z = e // 2, e % 2, d // 4, d % 4
    sibling = {"expert": y * 2 + 1 - c, "dp": d}

    def at_y(dy, core):
        return {"expert": ((y + dy) % 4) * 2 + core, "dp": d}

    def at_x(s):
        return {"expert": e, "dp": ((x + s) % 4) * 4 + z}

    def at_z(s):
        return {"expert": e, "dp": x * 4 + (z + s) % 4}

    bar = pltpu.get_barrier_semaphore()
    pl.semaphore_signal(bar, inc=1, device_id=sibling, device_id_type=MESH)
    for dy in (1, 2, 3):
        for core in (0, 1):
            pl.semaphore_signal(bar, inc=1, device_id=at_y(dy, core), device_id_type=MESH)
    for s in (1, 2, 3):
        pl.semaphore_signal(bar, inc=1, device_id=at_x(s), device_id_type=MESH)
        pl.semaphore_signal(bar, inc=1, device_id=at_z(s), device_id_type=MESH)
    load = pltpu.make_async_copy(tok_ref, tok.at[pl.ds(0, 8)], local_sem.at[0])
    load.start()
    own_g = pltpu.make_async_copy(gate_ref, wg.at[0, x, z], local_sem.at[1])
    own_u = pltpu.make_async_copy(up_ref, wu.at[0, x, z], local_sem.at[2])
    own_d = pltpu.make_async_copy(down_ref, down, local_sem.at[3])
    own_d.start()
    own_g.start()
    own_u.start()
    pl.semaphore_wait(bar, 13)

    def remote(src, dst, ss, rs, to):
        return pltpu.make_async_remote_copy(src_ref=src, dst_ref=dst, send_sem=ss, recv_sem=rs, device_id=to, device_id_type=MESH)

    def weights(m, k):
        out = []
        for s in (1, 2, 3):
            if k == 0:
                a, b = gate_ref if m == 0 else wg.at[m, x, z], up_ref if m == 0 else wu.at[m, x, z]
                out.append(remote(a, wg.at[m, x, z], w_ss.at[m, 0, 0, s - 1], w_rs.at[m, 0, 0, s - 1], at_x(s)))
                out.append(remote(b, wu.at[m, x, z], w_ss.at[m, 0, 1, s - 1], w_rs.at[m, 0, 1, s - 1], at_z(s)))
            elif k == 1 and s != 2:
                out.append(remote(wg.at[m, :, z], wg.at[m, :, z], w_ss.at[m, 1, 0, s - 1], w_rs.at[m, 1, 0, s - 1], at_z(s)))
                out.append(remote(wu.at[m, x], wu.at[m, x], w_ss.at[m, 1, 1, s - 1], w_rs.at[m, 1, 1, s - 1], at_x(s)))
            elif k == 2 and s != 2:
                half, fz, fx = pl.ds(s - 1, 2), (z + 4 - s) % 4, (x + 4 - s) % 4
                a, b = wg.at[m, half, fz], wu.at[m, fx, half]
                out.append(remote(a, a, w_ss.at[m, 2, 0, s - 1], w_rs.at[m, 2, 0, s - 1], at_z(s)))
                out.append(remote(b, b, w_ss.at[m, 2, 1, s - 1], w_rs.at[m, 2, 1, s - 1], at_x(s)))
        return out

    def shard():
        return [
            remote(gate_ref, wg.at[1, x, z], h_ss.at[0], h_rs.at[0], at_y(3, 0)),
            remote(up_ref, wu.at[1, x, z], h_ss.at[1], h_rs.at[1], at_y(3, 0)),
        ]

    def start(copies):
        for copy in copies:
            copy.start()

    def wait(copies):
        for copy in copies:
            copy.wait()

    start(weights(0, 0))

    @pl.when(c == 0)
    def _():
        start(shard())

    ids = [ids_ref[b] for b in range(8)]

    def slot(dy, core, second):
        want = ((y + dy) % 4) * 2 + core
        one = two = jnp.int32(8)
        for b in range(7, -1, -1):
            hit = ids[b] == want
            two = jnp.where(hit, one, two)
            one = jnp.where(hit, jnp.int32(b), one)
        return two if second else one

    tok[8] = jnp.zeros_like(tok[8])
    load.wait()

    def block_copy(n, k):
        dy, core, _, to, u = STEPS[n][k]
        return remote(send.at[n, k], got.at[u, c], tok_ss.at[n, k], tok_rs.at[u, c], at_y(to, core))

    def post(n):
        for k, b in enumerate(STEPS[n]):
            send[n, k] = tok[slot(*b[:3])]
            block_copy(n, k).start()

    def sent(n):
        for k in range(len(STEPS[n])):
            block_copy(n, k).wait_send()

    def near_copy(u, k):
        return remote(near.at[u // 2, k], got.at[u, k], near_ss.at[u // 2, k], tok_rs.at[u, k], sibling)

    for n in range(AHEAD):
        post(n)
    for k in range(2):
        near[0, k] = tok[slot(0, 1 - c, k)]
        near_copy(1, k).start()
        got[0, k] = tok[slot(0, c, k)]

    @pl.when(c == 0)
    def _():
        for k in range(2):
            got[2, k] = tok[slot(1, 0, k)]

    @pl.when(c == 1)
    def _():
        for k in range(2):
            near[1, k] = tok[slot(1, 0, k)]
            near_copy(3, k).start()

    acc[...] = jnp.zeros_like(acc)
    A[...] = jnp.zeros_like(A)
    R[...] = jnp.zeros_like(R)

    own_g.wait()
    own_u.wait()
    wait(weights(0, 0))
    start(weights(0, 1))

    @pl.when(c == 0)
    def _():
        wait(shard())
        start(weights(1, 0))

    @pl.when(c == 0)
    def _():
        wait(weights(1, 0))
        start(weights(1, 1))

    wait(weights(0, 1))
    start(weights(0, 2))

    for n in range(AHEAD, len(STEPS)):
        sent(n - AHEAD)
        post(n)
    for k in range(2):
        near_copy(1, k).wait_send()

    @pl.when(c == 1)
    def _():
        for k in range(2):
            near_copy(3, k).wait_send()

    @pl.when(c == 0)
    def _():
        wait(weights(1, 1))
        start(weights(1, 2))

    wait(weights(0, 2))
    model, width = 16 * wg.shape[3], wg.shape[4]

    def landed(u):
        for k in range(2):
            remote(near.at[0, k], got.at[u, k], near_ss.at[0, k], tok_rs.at[u, k], sibling).wait_recv()

    CA, CB = pl.ds(0, 512), pl.ds(512, 384)

    def at(r, n):
        return pl.ds(pl.multiple_of(r, 8), n)

    mine_a, mine_b = at(x * 32 + z * 8, 8), at(z * 32 + x * 8, 8)

    def fill(m, i):
        w = width - 128 * i
        top, low = i * 128, (5 - i) * 128
        pack[m, i, :, 0:w] = acc[m, top:top + 128, top:] * (1.0 / rows_avg)
        pack[m, i, :, w:] = acc[m, low:low + 128, low:] * (1.0 / rows_avg)

    def stage(m, i, k):
        out = []
        for s in (1, 2, 3):
            tx, tz = (x + s) % 4, (z + s) % 4
            if k == 0:
                a = pack.at[m, i, at(tx * 32, 32), CA], r1.at[m, i, s - 1, :, CA], at_x(s)
                b = pack.at[m, i, at(tz * 32, 32), CB], r1.at[m, i, s - 1, :, CB], at_z(s)
            elif k == 1:
                a = q1.at[m, i, at(tz * 8, 8), CA], r2.at[m, i, s - 1, :, CA], at_z(s)
                b = q1.at[m, i, at(tx * 8, 8), CB], r2.at[m, i, s - 1, :, CB], at_x(s)
            elif k == 2:
                a = q2.at[i, mine_a, CA], q2.at[i, mine_a, CA], at_z(s)
                b = q2.at[i, mine_b, CB], q2.at[i, mine_b, CB], at_x(s)
            else:
                a = q2.at[i, at(x * 32, 32), CA], q2.at[i, at(x * 32, 32), CA], at_x(s)
                b = q2.at[i, at(z * 32, 32), CB], q2.at[i, at(z * 32, 32), CB], at_z(s)
            for h, (src, dst, to) in enumerate((a, b)):
                out.append(remote(src, dst, g_ss.at[m, i, k, h, s - 1], g_rs.at[m, i, k, h, s - 1], to))
        return out

    def hop():
        return remote(bq, bs, h_ss.at[2], h_rs.at[2], at_y(1, 0))

    def begin(m, i, k):
        start(stage(m, i, k))

    def after(m, i, k):
        wait(stage(m, i, k))
        if k == 0:
            q1[m, i, :, CA] = (pack[m, i, at(x * 32, 32), CA] + r1[m, i, 0, :, CA]) + (r1[m, i, 1, :, CA] + r1[m, i, 2, :, CA])
            q1[m, i, :, CB] = (pack[m, i, at(z * 32, 32), CB] + r1[m, i, 0, :, CB]) + (r1[m, i, 1, :, CB] + r1[m, i, 2, :, CB])
        elif k == 1:
            a = (q1[m, i, at(z * 8, 8), CA] + r2[m, i, 0, :, CA]) + (r2[m, i, 1, :, CA] + r2[m, i, 2, :, CA])
            b = (q1[m, i, at(x * 8, 8), CB] + r2[m, i, 0, :, CB]) + (r2[m, i, 1, :, CB] + r2[m, i, 2, :, CB])
            if m == 1:
                bq[i, :, CA] = a
                bq[i, :, CB] = b
                return
            q2[i, mine_a, CA] = a
            q2[i, mine_b, CB] = b

            @pl.when(c == 0)
            def _():
                q2[i, mine_a, CA] += bs[i, :, CA]
                q2[i, mine_b, CB] += bs[i, :, CB]
        if k < 3:
            begin(m, i, k + 1)
            return
        same = lax.broadcasted_iota(jnp.int32, (128, 128), 0) == lax.broadcasted_iota(jnp.int32, (128, 128), 1)
        for b in (i, 5 - i):
            y0, w = b * 128, width - 128 * b
            lead = 0 if b < 3 else width + 128 - w
            A[y0:y0 + 128, y0:y0 + 128] += q2[i, :, lead:lead + 128] + jnp.where(same, damping, 0.0)
            if w > 128:
                A[y0:y0 + 128, y0 + 128:] += q2[i, :, lead + 128:lead + w]

    def unit(u, _):
        which = (1 - c) * (((u + 2) // 4) % 2)

        @pl.when((c == 0) & (u == 2))
        def _():
            wait(weights(1, 2))

        @pl.when((c == 0) & (u == 6))
        def _():
            for i in range(3):
                fill(1, i)
                begin(1, i, 0)

        @pl.when((c == 1) & (u == 2))
        def _():
            landed(2)

        for n in (1, 3, 4, 5, 6, 7):
            @pl.when(u == n)
            def _():
                landed(n)

        def part(n, _):
            cut = pl.ds(pl.multiple_of(n * 256, 256), 256)
            rows = got[u].reshape(PAIR, model)
            gate = jnp.dot(rows, wg[which, :, :, :, cut].reshape(model, 256), preferred_element_type=jnp.float32)
            lifted = jnp.dot(rows, wu[which, :, :, :, cut].reshape(model, 256), preferred_element_type=jnp.float32)
            hidden = gate / (1.0 + jnp.exp(-gate)) * lifted
            high = hidden.astype(jnp.bfloat16)
            low = (hidden - high.astype(jnp.float32)).astype(jnp.bfloat16)
            hid[0:256, cut] = high
            hid[256:512, cut] = high
            hid[512:768, cut] = low
            hid[768:1024, cut] = high
            return 0

        lax.fori_loop(0, width // 256, part, 0)

        @pl.when((c == 0) & (u == 7))
        def _():
            for i in range(3):
                after(1, i, 0)

        for i in range(0, width, 256):
            acc[which, i:i + 256, i:] += lax.dot_general(
                hid[0:768, i:i + 256], hid[256:1024, i:], (((0,), (0,)), ((), ())), preferred_element_type=jnp.float32
            )
        return 0

    lax.fori_loop(0, 8, unit, 0)
    fill(0, 0)
    begin(0, 0, 0)
    fill(0, 1)
    begin(0, 1, 0)

    @pl.when(c == 0)
    def _():
        for i in range(3):
            after(1, i, 1)
        hop().start()

    fill(0, 2)
    for n in range(len(STEPS) - AHEAD, len(STEPS)):
        sent(n)
    after(0, 0, 0)
    begin(0, 2, 0)

    @pl.when(c == 0)
    def _():
        hop().wait()

    after(0, 0, 1)
    after(0, 1, 0)
    after(0, 0, 2)
    after(0, 1, 1)
    after(0, 2, 0)
    after(0, 1, 2)
    after(0, 0, 3)

    def body(kb, _):
        row = pl.multiple_of(kb * 128, 128)
        for q in (1, 2):
            @pl.when(kb == q)
            def _():
                after(0, q, 3)

        blk = A[pl.ds(row, 128), pl.ds(row, 128)]
        up, lo = factor([blk[8 * t:8 * t + 8] for t in range(16)], 16)

        @pl.when(kb == 0)
        def _():
            after(0, 2, 1)

        for t in range(16):
            R[pl.ds(row + 8 * t, 8), pl.ds(row, 128)] = up[t]
            L[8 * t:8 * t + 8, :] = lo[t]
        for q in range(5):
            @pl.when(kb == q)
            def _():
                x0 = (q + 1) * 128
                panel = jnp.dot(L[...], A[q * 128:x0, x0:], precision=HI, preferred_element_type=jnp.float32)
                R[q * 128:x0, x0:] = panel
                if q == 0:
                    after(0, 2, 2)
                for i in range(q + 1, 6):
                    y0 = i * 128
                    A[y0:y0 + 128, y0:] -= lax.dot_general(
                        panel[:, y0 - x0:y0 - x0 + 128], panel[:, y0 - x0:], (((0,), (0,)), ((), ())), precision=HI,
                        preferred_element_type=jnp.float32,
                    )
        return 0

    lax.fori_loop(0, 6, body, 0)
    r_ref[...] = R[at(d * 48, 48), :]
    own_d.wait()
    for i in range(6):
        y0 = i * 128
        p_ref[y0:y0 + 128, :] = jnp.dot(
            R[y0:y0 + 128, y0:], down[y0:, :].astype(jnp.float32), precision=HI, preferred_element_type=jnp.float32
        )


def lanes(v, k):
    return jnp.take_along_axis(v, jnp.full((8, 128), k, jnp.int32), axis=1)


def subl(v, r):
    return jnp.broadcast_to(v[r:r + 1, :], (8, 128))


def factor(M, wide):
    M, tall = list(M), wide // 8
    lane = lax.broadcasted_iota(jnp.int32, (8, 128), 1)
    sub = lax.broadcasted_iota(jnp.int32, (8, 128), 0)
    zero = jnp.zeros((8, 128), jnp.float32)
    up, lo = [], []
    for q in range(0, 16, tall):
        k0 = 8 * q
        C = {t: [lanes(M[t], k0 + j) for j in range(wide)] for t in range(q, 16)}
        E = [[C[q + h][j] for h in range(tall)] for j in range(wide)]
        own = (lane >= k0) & (lane < k0 + wide)
        U = [M[q + h] for h in range(tall)]
        N = [jnp.where(own, (lane == sub + (k0 + 8 * h)).astype(jnp.float32), U[h]) for h in range(tall)]
        F = list(N)
        scale = [zero] * tall
        for j in range(0, wide, 2):
            g, r = divmod(j, 8)
            a, b, e = subl(E[j][g], r), subl(E[j + 1][g], r), subl(E[j + 1][g], r + 1)
            inv = 1.0 / (a * e - b * b)
            ia = 1.0 / a
            scale[g] = jnp.where(sub == r, ia, jnp.where(sub == r + 1, a * inv, scale[g]))
            ai, bi, ei = a * inv, b * inv, e * inv
            f0, f1, w0, w1 = [], [], [], []
            for h in range(tall):
                x0 = E[j][h] * ei - E[j + 1][h] * bi
                x1 = E[j + 1][h] * ai - E[j][h] * bi
                w0.append(x0 if h > g else jnp.where(sub > r + 1, x0, jnp.where(sub == r + 1, b * ia, 0.0)) if h == g else None)
                w1.append(x1 if h > g else jnp.where(sub > r + 1, x1, 0.0) if h == g else None)
                if h == g:
                    x0 = jnp.where(sub == r, -ei, jnp.where(sub == r + 1, bi, x0))
                    x1 = jnp.where(sub == r, bi, jnp.where(sub == r + 1, -ai, x1))
                f0.append(x0)
                f1.append(x1)
            pair = (sub == r) | (sub == r + 1)

            def jordan(V):
                p, s = subl(V[g], r), subl(V[g], r + 1)
                return [(jnp.where(pair, 0.0, V[h]) if h == g else V[h]) - (f0[h] * p + f1[h] * s) for h in range(tall)]

            def forward(V):
                p, s = subl(V[g], r), subl(V[g], r + 1)
                return [V[h] if h < g else V[h] - (w0[h] * p + w1[h] * s) for h in range(tall)]

            for i in range(j + 2, wide):
                E[i] = jordan(E[i])
            N, F, U = jordan(N), forward(F), forward(U)
        for h in range(tall):
            root = jnp.sqrt(scale[h])
            up.append(jnp.where(lane >= sub + (k0 + 8 * h), U[h] * root, 0.0))
            lo.append(jnp.where(lane <= sub + (k0 + 8 * h), F[h] * root, 0.0))
        G = [subl(N[j // 8], j % 8) for j in range(wide)]
        for t in range(q + tall, 16):
            terms = [C[t][j] * G[j] for j in range(wide)]
            while len(terms) > 1:
                terms = [terms[i] + terms[i + 1] for i in range(0, len(terms), 2)]
            M[t] = jnp.where(own, 0.0, M[t]) - terms[0]
    return up, lo


def factors(tokens, ids, gate, up, down, rows_avg):
    model, width = tokens.shape[1], gate.shape[1]
    any_, vmem = pl.BlockSpec(memory_space=pl.ANY), pl.BlockSpec(memory_space=pltpu.VMEM)
    bf, f32, dma = jnp.bfloat16, jnp.float32, pltpu.SemaphoreType.DMA
    return pl.pallas_call(
        functools.partial(whole_kernel, float(rows_avg)),
        out_shape=(pltpu.VMEM((width // 16, width), f32), pltpu.VMEM(down.shape, f32)),
        in_specs=[any_, pl.BlockSpec(memory_space=pltpu.SMEM), any_, any_, any_],
        out_specs=(vmem, vmem),
        scratch_shapes=[
            pltpu.VMEM((9, BROWS, model), bf),
            pltpu.VMEM((6, 2, BROWS, model), bf),
            pltpu.VMEM((2, 2, BROWS, model), bf),
            pltpu.VMEM((8, 2, BROWS, model), bf),
            pltpu.VMEM((2, 4, 4, model // 16, width), bf),
            pltpu.VMEM((2, 4, 4, model // 16, width), bf),
            pltpu.VMEM((4 * PAIR, width), bf),
            pltpu.VMEM((2, width, width), f32),
            pltpu.VMEM((2, 3, 128, width + 128), f32),
            pltpu.VMEM((2, 3, 3, 32, width + 128), f32),
            pltpu.VMEM((2, 3, 32, width + 128), f32),
            pltpu.VMEM((2, 3, 3, 8, width + 128), f32),
            pltpu.VMEM((3, 128, width + 128), f32),
            pltpu.VMEM((3, 8, width + 128), f32),
            pltpu.VMEM((3, 8, width + 128), f32),
            pltpu.VMEM(down.shape, bf),
            pltpu.VMEM((width, width), f32),
            pltpu.VMEM((width, width), f32),
            pltpu.VMEM((128, 128), f32),
            dma((4,)), dma((6, 2)), dma((2, 2)), dma((8, 2)), dma((2, 3, 2, 3)), dma((2, 3, 2, 3)), dma((3,)), dma((3,)),
            dma((2, 3, 4, 2, 3)), dma((2, 3, 4, 2, 3)),
        ],
        compiler_params=pltpu.CompilerParams(collective_id=1, has_side_effects=True, vmem_limit_bytes=60 << 20),
    )(tokens.reshape(8, BROWS, model), ids, gate, up, down)


def on_device(tokens, block_expert, gate_weight, up_weight, down_weight):
    rows_avg = tokens.shape[0] * lax.axis_size("expert") * lax.axis_size("dp") // lax.axis_size("expert")
    factor, product = factors(tokens, block_expert[:, 0], gate_weight[0], up_weight[0], down_weight[0], rows_avg)
    return (factor[None], product[None])


def solution(mesh):
    placed = (
        P(("expert", "dp"), None),
        P(("expert", "dp"), None),
        P("expert", "dp", None),
        P("expert", "dp", None),
        P("expert", None, "dp"),
    )
    return jax.shard_map(
        on_device,
        mesh=mesh,
        in_specs=placed,
        out_specs=(P("expert", "dp", None), P("expert", None, "dp")),
        check_vma=False,
    )
```

```python
import functools

import jax
import jax.numpy as jnp
from jax import lax
from jax.experimental import pallas as pl
from jax.experimental.pallas import tpu as pltpu
from jax.sharding import PartitionSpec as P

BROWS = 128
HI = lax.Precision.HIGHEST
damping = 0.05
MESH = pl.DeviceIdType.MESH
PAIR = 2 * BROWS
STEPS = (
    ((2, 1, 0, 2, 2),),
    ((2, 1, 1, 2, 3),),
    ((2, 0, 0, 1, 4), (3, 1, 0, 3, 4)),
    ((2, 0, 1, 1, 5), (3, 1, 1, 3, 5)),
    ((1, 1, 0, 1, 6), (3, 0, 0, 3, 6)),
    ((1, 1, 1, 1, 7), (3, 0, 1, 3, 7)),
)
AHEAD = 3


def whole_kernel(rows_avg, tok_ref, ids_ref, gate_ref, up_ref, down_ref, r_ref, p_ref,
                 tok, send, near, got, wg, wu, hid, acc, pack, r1, q1, r2, q2, bq, bs, down, A, R, L,
                 local_sem, tok_ss, near_ss, tok_rs, w_ss, w_rs, h_ss, h_rs, g_ss, g_rs):
    e, d = lax.axis_index("expert"), lax.axis_index("dp")
    y, c, x, z = e // 2, e % 2, d // 4, d % 4
    sibling = {"expert": y * 2 + 1 - c, "dp": d}

    def at_y(dy, core):
        return {"expert": ((y + dy) % 4) * 2 + core, "dp": d}

    def at_x(s):
        return {"expert": e, "dp": ((x + s) % 4) * 4 + z}

    def at_z(s):
        return {"expert": e, "dp": x * 4 + (z + s) % 4}

    bar = pltpu.get_barrier_semaphore()
    pl.semaphore_signal(bar, inc=1, device_id=sibling, device_id_type=MESH)
    for dy in (1, 2, 3):
        for core in (0, 1):
            pl.semaphore_signal(bar, inc=1, device_id=at_y(dy, core), device_id_type=MESH)
    for s in (1, 2, 3):
        pl.semaphore_signal(bar, inc=1, device_id=at_x(s), device_id_type=MESH)
        pl.semaphore_signal(bar, inc=1, device_id=at_z(s), device_id_type=MESH)
    load = pltpu.make_async_copy(tok_ref, tok.at[pl.ds(0, 8)], local_sem.at[0])
    load.start()
    own_g = pltpu.make_async_copy(gate_ref, wg.at[0, x, z], local_sem.at[1])
    own_u = pltpu.make_async_copy(up_ref, wu.at[0, x, z], local_sem.at[2])
    own_d = pltpu.make_async_copy(down_ref, down, local_sem.at[3])
    own_d.start()
    own_g.start()
    own_u.start()
    pl.semaphore_wait(bar, 13)

    def remote(src, dst, ss, rs, to):
        return pltpu.make_async_remote_copy(src_ref=src, dst_ref=dst, send_sem=ss, recv_sem=rs, device_id=to, device_id_type=MESH)

    def weights(m, k):
        out = []
        for s in (1, 2, 3):
            if k == 0:
                a, b = gate_ref if m == 0 else wg.at[m, x, z], up_ref if m == 0 else wu.at[m, x, z]
                out.append(remote(a, wg.at[m, x, z], w_ss.at[m, 0, 0, s - 1], w_rs.at[m, 0, 0, s - 1], at_x(s)))
                out.append(remote(b, wu.at[m, x, z], w_ss.at[m, 0, 1, s - 1], w_rs.at[m, 0, 1, s - 1], at_z(s)))
            elif k == 1 and s != 2:
                out.append(remote(wg.at[m, :, z], wg.at[m, :, z], w_ss.at[m, 1, 0, s - 1], w_rs.at[m, 1, 0, s - 1], at_z(s)))
                out.append(remote(wu.at[m, x], wu.at[m, x], w_ss.at[m, 1, 1, s - 1], w_rs.at[m, 1, 1, s - 1], at_x(s)))
            elif k == 2 and s != 2:
                half, fz, fx = pl.ds(s - 1, 2), (z + 4 - s) % 4, (x + 4 - s) % 4
                a, b = wg.at[m, half, fz], wu.at[m, fx, half]
                out.append(remote(a, a, w_ss.at[m, 2, 0, s - 1], w_rs.at[m, 2, 0, s - 1], at_z(s)))
                out.append(remote(b, b, w_ss.at[m, 2, 1, s - 1], w_rs.at[m, 2, 1, s - 1], at_x(s)))
        return out

    def shard():
        return [
            remote(gate_ref, wg.at[1, x, z], h_ss.at[0], h_rs.at[0], at_y(3, 0)),
            remote(up_ref, wu.at[1, x, z], h_ss.at[1], h_rs.at[1], at_y(3, 0)),
        ]

    def start(copies):
        for copy in copies:
            copy.start()

    def wait(copies):
        for copy in copies:
            copy.wait()

    start(weights(0, 0))

    @pl.when(c == 0)
    def _():
        start(shard())

    ids = [ids_ref[b] for b in range(8)]

    def slot(dy, core, second):
        want = ((y + dy) % 4) * 2 + core
        one = two = jnp.int32(8)
        for b in range(7, -1, -1):
            hit = ids[b] == want
            two = jnp.where(hit, one, two)
            one = jnp.where(hit, jnp.int32(b), one)
        return two if second else one

    tok[8] = jnp.zeros_like(tok[8])
    load.wait()

    def block_copy(n, k):
        dy, core, _, to, u = STEPS[n][k]
        return remote(send.at[n, k], got.at[u, c], tok_ss.at[n, k], tok_rs.at[u, c], at_y(to, core))

    def post(n):
        for k, b in enumerate(STEPS[n]):
            send[n, k] = tok[slot(*b[:3])]
            block_copy(n, k).start()

    def sent(n):
        for k in range(len(STEPS[n])):
            block_copy(n, k).wait_send()

    def near_copy(u, k):
        return remote(near.at[u // 2, k], got.at[u, k], near_ss.at[u // 2, k], tok_rs.at[u, k], sibling)

    for n in range(AHEAD):
        post(n)
    for k in range(2):
        near[0, k] = tok[slot(0, 1 - c, k)]
        near_copy(1, k).start()
        got[0, k] = tok[slot(0, c, k)]

    @pl.when(c == 0)
    def _():
        for k in range(2):
            got[2, k] = tok[slot(1, 0, k)]

    @pl.when(c == 1)
    def _():
        for k in range(2):
            near[1, k] = tok[slot(1, 0, k)]
            near_copy(3, k).start()

    acc[...] = jnp.zeros_like(acc)
    A[...] = jnp.zeros_like(A)
    R[...] = jnp.zeros_like(R)

    own_g.wait()
    own_u.wait()
    wait(weights(0, 0))
    start(weights(0, 1))

    @pl.when(c == 0)
    def _():
        wait(shard())
        start(weights(1, 0))

    @pl.when(c == 0)
    def _():
        wait(weights(1, 0))
        start(weights(1, 1))

    wait(weights(0, 1))
    start(weights(0, 2))

    for n in range(AHEAD, len(STEPS)):
        sent(n - AHEAD)
        post(n)
    for k in range(2):
        near_copy(1, k).wait_send()

    @pl.when(c == 1)
    def _():
        for k in range(2):
            near_copy(3, k).wait_send()

    @pl.when(c == 0)
    def _():
        wait(weights(1, 1))
        start(weights(1, 2))

    wait(weights(0, 2))
    model, width = 16 * wg.shape[3], wg.shape[4]

    def landed(u):
        for k in range(2):
            remote(near.at[0, k], got.at[u, k], near_ss.at[0, k], tok_rs.at[u, k], sibling).wait_recv()

    CA, CB = pl.ds(0, 512), pl.ds(512, 384)

    def at(r, n):
        return pl.ds(pl.multiple_of(r, 8), n)

    mine_a, mine_b = at(x * 32 + z * 8, 8), at(z * 32 + x * 8, 8)

    def fill(m, i):
        w = width - 128 * i
        top, low = i * 128, (5 - i) * 128
        pack[m, i, :, 0:w] = acc[m, top:top + 128, top:] * (1.0 / rows_avg)
        pack[m, i, :, w:] = acc[m, low:low + 128, low:] * (1.0 / rows_avg)

    def stage(m, i, k):
        out = []
        for s in (1, 2, 3):
            tx, tz = (x + s) % 4, (z + s) % 4
            if k == 0:
                a = pack.at[m, i, at(tx * 32, 32), CA], r1.at[m, i, s - 1, :, CA], at_x(s)
                b = pack.at[m, i, at(tz * 32, 32), CB], r1.at[m, i, s - 1, :, CB], at_z(s)
            elif k == 1:
                a = q1.at[m, i, at(tz * 8, 8), CA], r2.at[m, i, s - 1, :, CA], at_z(s)
                b = q1.at[m, i, at(tx * 8, 8), CB], r2.at[m, i, s - 1, :, CB], at_x(s)
            elif k == 2:
                a = q2.at[i, mine_a, CA], q2.at[i, mine_a, CA], at_z(s)
                b = q2.at[i, mine_b, CB], q2.at[i, mine_b, CB], at_x(s)
            else:
                a = q2.at[i, at(x * 32, 32), CA], q2.at[i, at(x * 32, 32), CA], at_x(s)
                b = q2.at[i, at(z * 32, 32), CB], q2.at[i, at(z * 32, 32), CB], at_z(s)
            for h, (src, dst, to) in enumerate((a, b)):
                out.append(remote(src, dst, g_ss.at[m, i, k, h, s - 1], g_rs.at[m, i, k, h, s - 1], to))
        return out

    def hop():
        return remote(bq, bs, h_ss.at[2], h_rs.at[2], at_y(1, 0))

    def begin(m, i, k):
        start(stage(m, i, k))

    def after(m, i, k):
        wait(stage(m, i, k))
        if k == 0:
            q1[m, i, :, CA] = (pack[m, i, at(x * 32, 32), CA] + r1[m, i, 0, :, CA]) + (r1[m, i, 1, :, CA] + r1[m, i, 2, :, CA])
            q1[m, i, :, CB] = (pack[m, i, at(z * 32, 32), CB] + r1[m, i, 0, :, CB]) + (r1[m, i, 1, :, CB] + r1[m, i, 2, :, CB])
        elif k == 1:
            a = (q1[m, i, at(z * 8, 8), CA] + r2[m, i, 0, :, CA]) + (r2[m, i, 1, :, CA] + r2[m, i, 2, :, CA])
            b = (q1[m, i, at(x * 8, 8), CB] + r2[m, i, 0, :, CB]) + (r2[m, i, 1, :, CB] + r2[m, i, 2, :, CB])
            if m == 1:
                bq[i, :, CA] = a
                bq[i, :, CB] = b
                return
            q2[i, mine_a, CA] = a
            q2[i, mine_b, CB] = b

            @pl.when(c == 0)
            def _():
                q2[i, mine_a, CA] += bs[i, :, CA]
                q2[i, mine_b, CB] += bs[i, :, CB]
        if k < 3:
            begin(m, i, k + 1)
            return
        same = lax.broadcasted_iota(jnp.int32, (128, 128), 0) == lax.broadcasted_iota(jnp.int32, (128, 128), 1)
        for b in (i, 5 - i):
            y0, w = b * 128, width - 128 * b
            lead = 0 if b < 3 else width + 128 - w
            A[y0:y0 + 128, y0:y0 + 128] += q2[i, :, lead:lead + 128] + jnp.where(same, damping, 0.0)
            if w > 128:
                A[y0:y0 + 128, y0 + 128:] += q2[i, :, lead + 128:lead + w]

    def unit(u, _):
        which = (1 - c) * (((u + 2) // 4) % 2)

        @pl.when((c == 0) & (u == 2))
        def _():
            wait(weights(1, 2))

        @pl.when((c == 0) & (u == 6))
        def _():
            for i in range(3):
                fill(1, i)
                begin(1, i, 0)

        @pl.when((c == 1) & (u == 2))
        def _():
            landed(2)

        for n in (1, 3, 4, 5, 6, 7):
            @pl.when(u == n)
            def _():
                landed(n)

        def part(n, _):
            cut = pl.ds(pl.multiple_of(n * 256, 256), 256)
            rows = got[u].reshape(PAIR, model)
            gate = jnp.dot(rows, wg[which, :, :, :, cut].reshape(model, 256), preferred_element_type=jnp.float32)
            lifted = jnp.dot(rows, wu[which, :, :, :, cut].reshape(model, 256), preferred_element_type=jnp.float32)
            hidden = gate / (1.0 + jnp.exp(-gate)) * lifted
            high = hidden.astype(jnp.bfloat16)
            low = (hidden - high.astype(jnp.float32)).astype(jnp.bfloat16)
            hid[0:256, cut] = high
            hid[256:512, cut] = high
            hid[512:768, cut] = low
            hid[768:1024, cut] = high
            return 0

        lax.fori_loop(0, width // 256, part, 0)

        @pl.when((c == 0) & (u == 7))
        def _():
            for i in range(3):
                after(1, i, 0)

        for i in range(0, width, 256):
            acc[which, i:i + 256, i:] += lax.dot_general(
                hid[0:768, i:i + 256], hid[256:1024, i:], (((0,), (0,)), ((), ())), preferred_element_type=jnp.float32
            )
        return 0

    lax.fori_loop(0, 8, unit, 0)
    fill(0, 0)
    begin(0, 0, 0)
    fill(0, 1)
    begin(0, 1, 0)

    @pl.when(c == 0)
    def _():
        for i in range(3):
            after(1, i, 1)
        hop().start()

    fill(0, 2)
    for n in range(len(STEPS) - AHEAD, len(STEPS)):
        sent(n)
    after(0, 0, 0)
    begin(0, 2, 0)

    @pl.when(c == 0)
    def _():
        hop().wait()

    after(0, 0, 1)
    after(0, 1, 0)
    after(0, 0, 2)
    after(0, 1, 1)
    after(0, 2, 0)
    after(0, 1, 2)
    after(0, 2, 1)
    after(0, 0, 3)

    own_d.wait()

    def product(i):
        y0 = i * 128
        p_ref[y0:y0 + 128, :] = jnp.dot(
            R[y0:y0 + 128, y0:], down[y0:, :].astype(jnp.float32), precision=HI, preferred_element_type=jnp.float32
        )

    def body(kb, _):
        row = pl.multiple_of(kb * 128, 128)
        for q in (1, 2):
            @pl.when(kb == q)
            def _():
                after(0, q, 3)

        blk = A[pl.ds(row, 128), pl.ds(row, 128)]
        up, lo = factor([blk[8 * t:8 * t + 8] for t in range(16)], 16)

        @pl.when(kb == 0)
        def _():
            after(0, 2, 2)

        for t in range(16):
            R[pl.ds(row + 8 * t, 8), pl.ds(row, 128)] = up[t]
            L[8 * t:8 * t + 8, :] = lo[t]
        for q in range(5):
            @pl.when(kb == q)
            def _():
                x0 = (q + 1) * 128
                panel = jnp.dot(L[...], A[q * 128:x0, x0:], precision=HI, preferred_element_type=jnp.float32)
                R[q * 128:x0, x0:] = panel
                product(q)
                for i in range(q + 1, 6):
                    y0 = i * 128
                    A[y0:y0 + 128, y0:] -= lax.dot_general(
                        panel[:, y0 - x0:y0 - x0 + 128], panel[:, y0 - x0:], (((0,), (0,)), ((), ())), precision=HI,
                        preferred_element_type=jnp.float32,
                    )
        return 0

    lax.fori_loop(0, 6, body, 0)
    product(5)
    r_ref[...] = R[at(d * 48, 48), :]


def lanes(v, k):
    return jnp.take_along_axis(v, jnp.full((8, 128), k, jnp.int32), axis=1)


def subl(v, r):
    return jnp.broadcast_to(v[r:r + 1, :], (8, 128))


def factor(M, wide):
    M, tall = list(M), wide // 8
    lane = lax.broadcasted_iota(jnp.int32, (8, 128), 1)
    sub = lax.broadcasted_iota(jnp.int32, (8, 128), 0)
    zero = jnp.zeros((8, 128), jnp.float32)
    up, lo = [], []
    for q in range(0, 16, tall):
        k0 = 8 * q
        C = {t: [lanes(M[t], k0 + j) for j in range(wide)] for t in range(q, 16)}
        E = [[C[q + h][j] for h in range(tall)] for j in range(wide)]
        own = (lane >= k0) & (lane < k0 + wide)
        U = [M[q + h] for h in range(tall)]
        N = [jnp.where(own, (lane == sub + (k0 + 8 * h)).astype(jnp.float32), U[h]) for h in range(tall)]
        F = list(N)
        scale = [zero] * tall
        for j in range(0, wide, 2):
            g, r = divmod(j, 8)
            a, b, e = subl(E[j][g], r), subl(E[j + 1][g], r), subl(E[j + 1][g], r + 1)
            inv = 1.0 / (a * e - b * b)
            ia = 1.0 / a
            scale[g] = jnp.where(sub == r, ia, jnp.where(sub == r + 1, a * inv, scale[g]))
            ai, bi, ei = a * inv, b * inv, e * inv
            f0, f1, w0, w1 = [], [], [], []
            for h in range(tall):
                x0 = E[j][h] * ei - E[j + 1][h] * bi
                x1 = E[j + 1][h] * ai - E[j][h] * bi
                w0.append(x0 if h > g else jnp.where(sub > r + 1, x0, jnp.where(sub == r + 1, b * ia, 0.0)) if h == g else None)
                w1.append(x1 if h > g else jnp.where(sub > r + 1, x1, 0.0) if h == g else None)
                if h == g:
                    x0 = jnp.where(sub == r, -ei, jnp.where(sub == r + 1, bi, x0))
                    x1 = jnp.where(sub == r, bi, jnp.where(sub == r + 1, -ai, x1))
                f0.append(x0)
                f1.append(x1)
            pair = (sub == r) | (sub == r + 1)

            def jordan(V):
                p, s = subl(V[g], r), subl(V[g], r + 1)
                return [(jnp.where(pair, 0.0, V[h]) if h == g else V[h]) - (f0[h] * p + f1[h] * s) for h in range(tall)]

            def forward(V):
                p, s = subl(V[g], r), subl(V[g], r + 1)
                return [V[h] if h < g else V[h] - (w0[h] * p + w1[h] * s) for h in range(tall)]

            for i in range(j + 2, wide):
                E[i] = jordan(E[i])
            N, F, U = jordan(N), forward(F), forward(U)
        for h in range(tall):
            root = jnp.sqrt(scale[h])
            up.append(jnp.where(lane >= sub + (k0 + 8 * h), U[h] * root, 0.0))
            lo.append(jnp.where(lane <= sub + (k0 + 8 * h), F[h] * root, 0.0))
        G = [subl(N[j // 8], j % 8) for j in range(wide)]
        for t in range(q + tall, 16):
            terms = [C[t][j] * G[j] for j in range(wide)]
            while len(terms) > 1:
                terms = [terms[i] + terms[i + 1] for i in range(0, len(terms), 2)]
            M[t] = jnp.where(own, 0.0, M[t]) - terms[0]
    return up, lo


def factors(tokens, ids, gate, up, down, rows_avg):
    model, width = tokens.shape[1], gate.shape[1]
    any_, vmem = pl.BlockSpec(memory_space=pl.ANY), pl.BlockSpec(memory_space=pltpu.VMEM)
    bf, f32, dma = jnp.bfloat16, jnp.float32, pltpu.SemaphoreType.DMA
    return pl.pallas_call(
        functools.partial(whole_kernel, float(rows_avg)),
        out_shape=(pltpu.VMEM((width // 16, width), f32), pltpu.VMEM(down.shape, f32)),
        in_specs=[any_, pl.BlockSpec(memory_space=pltpu.SMEM), any_, any_, any_],
        out_specs=(vmem, vmem),
        scratch_shapes=[
            pltpu.VMEM((9, BROWS, model), bf),
            pltpu.VMEM((6, 2, BROWS, model), bf),
            pltpu.VMEM((2, 2, BROWS, model), bf),
            pltpu.VMEM((8, 2, BROWS, model), bf),
            pltpu.VMEM((2, 4, 4, model // 16, width), bf),
            pltpu.VMEM((2, 4, 4, model // 16, width), bf),
            pltpu.VMEM((4 * PAIR, width), bf),
            pltpu.VMEM((2, width, width), f32),
            pltpu.VMEM((2, 3, 128, width + 128), f32),
            pltpu.VMEM((2, 3, 3, 32, width + 128), f32),
            pltpu.VMEM((2, 3, 32, width + 128), f32),
            pltpu.VMEM((2, 3, 3, 8, width + 128), f32),
            pltpu.VMEM((3, 128, width + 128), f32),
            pltpu.VMEM((3, 8, width + 128), f32),
            pltpu.VMEM((3, 8, width + 128), f32),
            pltpu.VMEM(down.shape, bf),
            pltpu.VMEM((width, width), f32),
            pltpu.VMEM((width, width), f32),
            pltpu.VMEM((128, 128), f32),
            dma((4,)), dma((6, 2)), dma((2, 2)), dma((8, 2)), dma((2, 3, 2, 3)), dma((2, 3, 2, 3)), dma((3,)), dma((3,)),
            dma((2, 3, 4, 2, 3)), dma((2, 3, 4, 2, 3)),
        ],
        compiler_params=pltpu.CompilerParams(collective_id=1, has_side_effects=True, vmem_limit_bytes=60 << 20),
    )(tokens.reshape(8, BROWS, model), ids, gate, up, down)


def on_device(tokens, block_expert, gate_weight, up_weight, down_weight):
    rows_avg = tokens.shape[0] * lax.axis_size("expert") * lax.axis_size("dp") // lax.axis_size("expert")
    factor, product = factors(tokens, block_expert[:, 0], gate_weight[0], up_weight[0], down_weight[0], rows_avg)
    return (factor[None], product[None])


def solution(mesh):
    placed = (
        P(("expert", "dp"), None),
        P(("expert", "dp"), None),
        P("expert", "dp", None),
        P("expert", "dp", None),
        P("expert", None, "dp"),
    )
    return jax.shard_map(
        on_device,
        mesh=mesh,
        in_specs=placed,
        out_specs=(P("expert", "dp", None), P("expert", None, "dp")),
        check_vma=False,
    )
```

```python
import functools

import jax
import jax.numpy as jnp
from jax import lax
from jax.experimental import pallas as pl
from jax.experimental.pallas import tpu as pltpu
from jax.sharding import PartitionSpec as P

BROWS = 128
HI = lax.Precision.HIGHEST
damping = 0.05
MESH = pl.DeviceIdType.MESH
PAIR = 2 * BROWS
STEPS = (
    ((2, 1, 0, 2, 2),),
    ((2, 1, 1, 2, 3),),
    ((2, 0, 0, 1, 4), (3, 1, 0, 3, 4)),
    ((2, 0, 1, 1, 5), (3, 1, 1, 3, 5)),
    ((1, 1, 0, 1, 6), (3, 0, 0, 3, 6)),
    ((1, 1, 1, 1, 7), (3, 0, 1, 3, 7)),
)
AHEAD = 4


def whole_kernel(rows_avg, tok_ref, ids_ref, gate_ref, up_ref, down_ref, r_ref, p_ref,
                 tok, send, near, got, wg, wu, hid, acc, pack, r1, q1, r2, q2, bq, bs, down, A, R, L,
                 local_sem, tok_ss, near_ss, tok_rs, w_ss, w_rs, h_ss, h_rs, g_ss, g_rs):
    e, d = lax.axis_index("expert"), lax.axis_index("dp")
    y, c, x, z = e // 2, e % 2, d // 4, d % 4
    sibling = {"expert": y * 2 + 1 - c, "dp": d}

    def at_y(dy, core):
        return {"expert": ((y + dy) % 4) * 2 + core, "dp": d}

    def at_x(s):
        return {"expert": e, "dp": ((x + s) % 4) * 4 + z}

    def at_z(s):
        return {"expert": e, "dp": x * 4 + (z + s) % 4}

    bar = pltpu.get_barrier_semaphore()
    pl.semaphore_signal(bar, inc=1, device_id=sibling, device_id_type=MESH)
    for dy in (1, 2, 3):
        for core in (0, 1):
            pl.semaphore_signal(bar, inc=1, device_id=at_y(dy, core), device_id_type=MESH)
    for s in (1, 2, 3):
        pl.semaphore_signal(bar, inc=1, device_id=at_x(s), device_id_type=MESH)
        pl.semaphore_signal(bar, inc=1, device_id=at_z(s), device_id_type=MESH)
    load = pltpu.make_async_copy(tok_ref, tok.at[pl.ds(0, 8)], local_sem.at[0])
    load.start()
    own_g = pltpu.make_async_copy(gate_ref, wg.at[0, x, z], local_sem.at[1])
    own_u = pltpu.make_async_copy(up_ref, wu.at[0, x, z], local_sem.at[2])
    own_d = pltpu.make_async_copy(down_ref, down, local_sem.at[3])
    own_d.start()
    own_g.start()
    own_u.start()
    pl.semaphore_wait(bar, 13)

    def remote(src, dst, ss, rs, to):
        return pltpu.make_async_remote_copy(src_ref=src, dst_ref=dst, send_sem=ss, recv_sem=rs, device_id=to, device_id_type=MESH)

    def weights(m, k):
        out = []
        for s in (1, 2, 3):
            if k == 0:
                a, b = gate_ref if m == 0 else wg.at[m, x, z], up_ref if m == 0 else wu.at[m, x, z]
                out.append(remote(a, wg.at[m, x, z], w_ss.at[m, 0, 0, s - 1], w_rs.at[m, 0, 0, s - 1], at_x(s)))
                out.append(remote(b, wu.at[m, x, z], w_ss.at[m, 0, 1, s - 1], w_rs.at[m, 0, 1, s - 1], at_z(s)))
            elif k == 1 and s != 2:
                out.append(remote(wg.at[m, :, z], wg.at[m, :, z], w_ss.at[m, 1, 0, s - 1], w_rs.at[m, 1, 0, s - 1], at_z(s)))
                out.append(remote(wu.at[m, x], wu.at[m, x], w_ss.at[m, 1, 1, s - 1], w_rs.at[m, 1, 1, s - 1], at_x(s)))
            elif k == 2 and s != 2:
                half, fz, fx = pl.ds(s - 1, 2), (z + 4 - s) % 4, (x + 4 - s) % 4
                a, b = wg.at[m, half, fz], wu.at[m, fx, half]
                out.append(remote(a, a, w_ss.at[m, 2, 0, s - 1], w_rs.at[m, 2, 0, s - 1], at_z(s)))
                out.append(remote(b, b, w_ss.at[m, 2, 1, s - 1], w_rs.at[m, 2, 1, s - 1], at_x(s)))
        return out

    def shard():
        return [
            remote(gate_ref, wg.at[1, x, z], h_ss.at[0], h_rs.at[0], at_y(3, 0)),
            remote(up_ref, wu.at[1, x, z], h_ss.at[1], h_rs.at[1], at_y(3, 0)),
        ]

    def start(copies):
        for copy in copies:
            copy.start()

    def wait(copies):
        for copy in copies:
            copy.wait()

    start(weights(0, 0))

    @pl.when(c == 0)
    def _():
        start(shard())

    ids = [ids_ref[b] for b in range(8)]

    def slot(dy, core, second):
        want = ((y + dy) % 4) * 2 + core
        one = two = jnp.int32(8)
        for b in range(7, -1, -1):
            hit = ids[b] == want
            two = jnp.where(hit, one, two)
            one = jnp.where(hit, jnp.int32(b), one)
        return two if second else one

    tok[8] = jnp.zeros_like(tok[8])
    load.wait()

    def block_copy(n, k):
        dy, core, _, to, u = STEPS[n][k]
        return remote(send.at[n, k], got.at[u, c], tok_ss.at[n, k], tok_rs.at[u, c], at_y(to, core))

    def post(n):
        for k, b in enumerate(STEPS[n]):
            send[n, k] = tok[slot(*b[:3])]
            block_copy(n, k).start()

    def sent(n):
        for k in range(len(STEPS[n])):
            block_copy(n, k).wait_send()

    def near_copy(u, k):
        return remote(near.at[u // 2, k], got.at[u, k], near_ss.at[u // 2, k], tok_rs.at[u, k], sibling)

    for n in range(AHEAD):
        post(n)
    for k in range(2):
        near[0, k] = tok[slot(0, 1 - c, k)]
        near_copy(1, k).start()
        got[0, k] = tok[slot(0, c, k)]

    @pl.when(c == 0)
    def _():
        for k in range(2):
            got[2, k] = tok[slot(1, 0, k)]

    @pl.when(c == 1)
    def _():
        for k in range(2):
            near[1, k] = tok[slot(1, 0, k)]
            near_copy(3, k).start()

    acc[...] = jnp.zeros_like(acc)
    A[...] = jnp.zeros_like(A)
    R[...] = jnp.zeros_like(R)

    own_g.wait()
    own_u.wait()
    wait(weights(0, 0))
    start(weights(0, 1))

    @pl.when(c == 0)
    def _():
        wait(shard())
        start(weights(1, 0))

    @pl.when(c == 0)
    def _():
        wait(weights(1, 0))
        start(weights(1, 1))

    wait(weights(0, 1))
    start(weights(0, 2))

    for n in range(AHEAD, len(STEPS)):
        sent(n - AHEAD)
        post(n)
    for k in range(2):
        near_copy(1, k).wait_send()

    @pl.when(c == 1)
    def _():
        for k in range(2):
            near_copy(3, k).wait_send()

    @pl.when(c == 0)
    def _():
        wait(weights(1, 1))
        start(weights(1, 2))

    wait(weights(0, 2))
    model, width = 16 * wg.shape[3], wg.shape[4]

    def landed(u):
        for k in range(2):
            remote(near.at[0, k], got.at[u, k], near_ss.at[0, k], tok_rs.at[u, k], sibling).wait_recv()

    CA, CB = pl.ds(0, 512), pl.ds(512, 384)

    def at(r, n):
        return pl.ds(pl.multiple_of(r, 8), n)

    mine_a, mine_b = at(x * 32 + z * 8, 8), at(z * 32 + x * 8, 8)

    def fill(m, i):
        w = width - 128 * i
        top, low = i * 128, (5 - i) * 128
        pack[m, i, :, 0:w] = acc[m, top:top + 128, top:] * (1.0 / rows_avg)
        pack[m, i, :, w:] = acc[m, low:low + 128, low:] * (1.0 / rows_avg)

    def stage(m, i, k):
        out = []
        for s in (1, 2, 3):
            tx, tz = (x + s) % 4, (z + s) % 4
            if k == 0:
                a = pack.at[m, i, at(tx * 32, 32), CA], r1.at[m, i, s - 1, :, CA], at_x(s)
                b = pack.at[m, i, at(tz * 32, 32), CB], r1.at[m, i, s - 1, :, CB], at_z(s)
            elif k == 1:
                a = q1.at[m, i, at(tz * 8, 8), CA], r2.at[m, i, s - 1, :, CA], at_z(s)
                b = q1.at[m, i, at(tx * 8, 8), CB], r2.at[m, i, s - 1, :, CB], at_x(s)
            elif k == 2:
                a = q2.at[i, mine_a, CA], q2.at[i, mine_a, CA], at_z(s)
                b = q2.at[i, mine_b, CB], q2.at[i, mine_b, CB], at_x(s)
            else:
                a = q2.at[i, at(x * 32, 32), CA], q2.at[i, at(x * 32, 32), CA], at_x(s)
                b = q2.at[i, at(z * 32, 32), CB], q2.at[i, at(z * 32, 32), CB], at_z(s)
            for h, (src, dst, to) in enumerate((a, b)):
                out.append(remote(src, dst, g_ss.at[m, i, k, h, s - 1], g_rs.at[m, i, k, h, s - 1], to))
        return out

    def hop():
        return remote(bq, bs, h_ss.at[2], h_rs.at[2], at_y(1, 0))

    def begin(m, i, k):
        start(stage(m, i, k))

    def after(m, i, k):
        wait(stage(m, i, k))
        if k == 0:
            q1[m, i, :, CA] = (pack[m, i, at(x * 32, 32), CA] + r1[m, i, 0, :, CA]) + (r1[m, i, 1, :, CA] + r1[m, i, 2, :, CA])
            q1[m, i, :, CB] = (pack[m, i, at(z * 32, 32), CB] + r1[m, i, 0, :, CB]) + (r1[m, i, 1, :, CB] + r1[m, i, 2, :, CB])
        elif k == 1:
            a = (q1[m, i, at(z * 8, 8), CA] + r2[m, i, 0, :, CA]) + (r2[m, i, 1, :, CA] + r2[m, i, 2, :, CA])
            b = (q1[m, i, at(x * 8, 8), CB] + r2[m, i, 0, :, CB]) + (r2[m, i, 1, :, CB] + r2[m, i, 2, :, CB])
            if m == 1:
                bq[i, :, CA] = a
                bq[i, :, CB] = b
                return
            q2[i, mine_a, CA] = a
            q2[i, mine_b, CB] = b

            @pl.when(c == 0)
            def _():
                q2[i, mine_a, CA] += bs[i, :, CA]
                q2[i, mine_b, CB] += bs[i, :, CB]
        if k < 3:
            begin(m, i, k + 1)
            return
        same = lax.broadcasted_iota(jnp.int32, (128, 128), 0) == lax.broadcasted_iota(jnp.int32, (128, 128), 1)
        for b in (i, 5 - i):
            y0, w = b * 128, width - 128 * b
            lead = 0 if b < 3 else width + 128 - w
            A[y0:y0 + 128, y0:y0 + 128] += q2[i, :, lead:lead + 128] + jnp.where(same, damping, 0.0)
            if w > 128:
                A[y0:y0 + 128, y0 + 128:] += q2[i, :, lead + 128:lead + w]

    def unit(u, _):
        which = (1 - c) * (((u + 2) // 4) % 2)

        @pl.when((c == 0) & (u == 2))
        def _():
            wait(weights(1, 2))

        @pl.when((c == 0) & (u == 6))
        def _():
            for i in range(3):
                fill(1, i)
                begin(1, i, 0)

        @pl.when((c == 1) & (u == 2))
        def _():
            landed(2)

        for n in (1, 3, 4, 5, 6, 7):
            @pl.when(u == n)
            def _():
                landed(n)

        def part(n, _):
            cut = pl.ds(pl.multiple_of(n * 256, 256), 256)
            rows = got[u].reshape(PAIR, model)
            gate = jnp.dot(rows, wg[which, :, :, :, cut].reshape(model, 256), preferred_element_type=jnp.float32)
            lifted = jnp.dot(rows, wu[which, :, :, :, cut].reshape(model, 256), preferred_element_type=jnp.float32)
            hidden = gate / (1.0 + jnp.exp(-gate)) * lifted
            high = hidden.astype(jnp.bfloat16)
            low = (hidden - high.astype(jnp.float32)).astype(jnp.bfloat16)
            hid[0:256, cut] = high
            hid[256:512, cut] = high
            hid[512:768, cut] = low
            hid[768:1024, cut] = high
            return 0

        lax.fori_loop(0, width // 256, part, 0)

        @pl.when((c == 0) & (u == 7))
        def _():
            for i in range(3):
                after(1, i, 0)

        for i in range(0, width, 256):
            acc[which, i:i + 256, i:] += lax.dot_general(
                hid[0:768, i:i + 256], hid[256:1024, i:], (((0,), (0,)), ((), ())), preferred_element_type=jnp.float32
            )
        return 0

    lax.fori_loop(0, 8, unit, 0)
    fill(0, 0)
    begin(0, 0, 0)
    fill(0, 1)
    begin(0, 1, 0)

    @pl.when(c == 0)
    def _():
        for i in range(3):
            after(1, i, 1)
        hop().start()

    fill(0, 2)
    for n in range(len(STEPS) - AHEAD, len(STEPS)):
        sent(n)
    after(0, 0, 0)
    begin(0, 2, 0)

    @pl.when(c == 0)
    def _():
        hop().wait()

    after(0, 0, 1)
    after(0, 1, 0)
    after(0, 0, 2)
    after(0, 1, 1)
    after(0, 2, 0)
    after(0, 1, 2)
    after(0, 2, 1)
    after(0, 0, 3)

    own_d.wait()

    def product(i):
        y0 = i * 128
        p_ref[y0:y0 + 128, :] = jnp.dot(
            R[y0:y0 + 128, y0:], down[y0:, :].astype(jnp.float32), precision=HI, preferred_element_type=jnp.float32
        )

    def body(kb, _):
        row = pl.multiple_of(kb * 128, 128)
        for q in (1, 2):
            @pl.when(kb == q)
            def _():
                after(0, q, 3)

        blk = A[pl.ds(row, 128), pl.ds(row, 128)]
        up, lo = factor([blk[8 * t:8 * t + 8] for t in range(16)], 16)

        @pl.when(kb == 0)
        def _():
            after(0, 2, 2)

        for t in range(16):
            R[pl.ds(row + 8 * t, 8), pl.ds(row, 128)] = up[t]
            L[8 * t:8 * t + 8, :] = lo[t]
        for q in range(5):
            @pl.when(kb == q)
            def _():
                x0 = (q + 1) * 128
                panel = jnp.dot(L[...], A[q * 128:x0, x0:], precision=HI, preferred_element_type=jnp.float32)
                R[q * 128:x0, x0:] = panel
                product(q)
                for i in range(q + 1, 6):
                    y0 = i * 128
                    A[y0:y0 + 128, y0:] -= lax.dot_general(
                        panel[:, y0 - x0:y0 - x0 + 128], panel[:, y0 - x0:], (((0,), (0,)), ((), ())), precision=HI,
                        preferred_element_type=jnp.float32,
                    )
        return 0

    lax.fori_loop(0, 6, body, 0)
    product(5)
    r_ref[...] = R[at(d * 48, 48), :]


def lanes(v, k):
    return jnp.take_along_axis(v, jnp.full((8, 128), k, jnp.int32), axis=1)


def subl(v, r):
    return jnp.broadcast_to(v[r:r + 1, :], (8, 128))


def factor(M, wide):
    M, tall = list(M), wide // 8
    lane = lax.broadcasted_iota(jnp.int32, (8, 128), 1)
    sub = lax.broadcasted_iota(jnp.int32, (8, 128), 0)
    zero = jnp.zeros((8, 128), jnp.float32)
    up, lo = [], []
    for q in range(0, 16, tall):
        k0 = 8 * q
        C = {t: [lanes(M[t], k0 + j) for j in range(wide)] for t in range(q, 16)}
        E = [[C[q + h][j] for h in range(tall)] for j in range(wide)]
        own = (lane >= k0) & (lane < k0 + wide)
        U = [M[q + h] for h in range(tall)]
        N = [jnp.where(own, (lane == sub + (k0 + 8 * h)).astype(jnp.float32), U[h]) for h in range(tall)]
        F = list(N)
        scale = [zero] * tall
        for j in range(0, wide, 2):
            g, r = divmod(j, 8)
            a, b, e = subl(E[j][g], r), subl(E[j + 1][g], r), subl(E[j + 1][g], r + 1)
            inv = 1.0 / (a * e - b * b)
            ia = 1.0 / a
            scale[g] = jnp.where(sub == r, ia, jnp.where(sub == r + 1, a * inv, scale[g]))
            ai, bi, ei = a * inv, b * inv, e * inv
            f0, f1, w0, w1 = [], [], [], []
            for h in range(tall):
                x0 = E[j][h] * ei - E[j + 1][h] * bi
                x1 = E[j + 1][h] * ai - E[j][h] * bi
                w0.append(x0 if h > g else jnp.where(sub > r + 1, x0, jnp.where(sub == r + 1, b * ia, 0.0)) if h == g else None)
                w1.append(x1 if h > g else jnp.where(sub > r + 1, x1, 0.0) if h == g else None)
                if h == g:
                    x0 = jnp.where(sub == r, -ei, jnp.where(sub == r + 1, bi, x0))
                    x1 = jnp.where(sub == r, bi, jnp.where(sub == r + 1, -ai, x1))
                f0.append(x0)
                f1.append(x1)
            pair = (sub == r) | (sub == r + 1)

            def jordan(V):
                p, s = subl(V[g], r), subl(V[g], r + 1)
                return [(jnp.where(pair, 0.0, V[h]) if h == g else V[h]) - (f0[h] * p + f1[h] * s) for h in range(tall)]

            def forward(V):
                p, s = subl(V[g], r), subl(V[g], r + 1)
                return [V[h] if h < g else V[h] - (w0[h] * p + w1[h] * s) for h in range(tall)]

            for i in range(j + 2, wide):
                E[i] = jordan(E[i])
            N, F, U = jordan(N), forward(F), forward(U)
        for h in range(tall):
            root = jnp.sqrt(scale[h])
            up.append(jnp.where(lane >= sub + (k0 + 8 * h), U[h] * root, 0.0))
            lo.append(jnp.where(lane <= sub + (k0 + 8 * h), F[h] * root, 0.0))
        G = [subl(N[j // 8], j % 8) for j in range(wide)]
        for t in range(q + tall, 16):
            terms = [C[t][j] * G[j] for j in range(wide)]
            while len(terms) > 1:
                terms = [terms[i] + terms[i + 1] for i in range(0, len(terms), 2)]
            M[t] = jnp.where(own, 0.0, M[t]) - terms[0]
    return up, lo


def factors(tokens, ids, gate, up, down, rows_avg):
    model, width = tokens.shape[1], gate.shape[1]
    any_, vmem = pl.BlockSpec(memory_space=pl.ANY), pl.BlockSpec(memory_space=pltpu.VMEM)
    bf, f32, dma = jnp.bfloat16, jnp.float32, pltpu.SemaphoreType.DMA
    return pl.pallas_call(
        functools.partial(whole_kernel, float(rows_avg)),
        out_shape=(pltpu.VMEM((width // 16, width), f32), pltpu.VMEM(down.shape, f32)),
        in_specs=[any_, pl.BlockSpec(memory_space=pltpu.SMEM), any_, any_, any_],
        out_specs=(vmem, vmem),
        scratch_shapes=[
            pltpu.VMEM((9, BROWS, model), bf),
            pltpu.VMEM((6, 2, BROWS, model), bf),
            pltpu.VMEM((2, 2, BROWS, model), bf),
            pltpu.VMEM((8, 2, BROWS, model), bf),
            pltpu.VMEM((2, 4, 4, model // 16, width), bf),
            pltpu.VMEM((2, 4, 4, model // 16, width), bf),
            pltpu.VMEM((4 * PAIR, width), bf),
            pltpu.VMEM((2, width, width), f32),
            pltpu.VMEM((2, 3, 128, width + 128), f32),
            pltpu.VMEM((2, 3, 3, 32, width + 128), f32),
            pltpu.VMEM((2, 3, 32, width + 128), f32),
            pltpu.VMEM((2, 3, 3, 8, width + 128), f32),
            pltpu.VMEM((3, 128, width + 128), f32),
            pltpu.VMEM((3, 8, width + 128), f32),
            pltpu.VMEM((3, 8, width + 128), f32),
            pltpu.VMEM(down.shape, bf),
            pltpu.VMEM((width, width), f32),
            pltpu.VMEM((width, width), f32),
            pltpu.VMEM((128, 128), f32),
            dma((4,)), dma((6, 2)), dma((2, 2)), dma((8, 2)), dma((2, 3, 2, 3)), dma((2, 3, 2, 3)), dma((3,)), dma((3,)),
            dma((2, 3, 4, 2, 3)), dma((2, 3, 4, 2, 3)),
        ],
        compiler_params=pltpu.CompilerParams(collective_id=1, has_side_effects=True, vmem_limit_bytes=60 << 20),
    )(tokens.reshape(8, BROWS, model), ids, gate, up, down)


def on_device(tokens, block_expert, gate_weight, up_weight, down_weight):
    rows_avg = tokens.shape[0] * lax.axis_size("expert") * lax.axis_size("dp") // lax.axis_size("expert")
    factor, product = factors(tokens, block_expert[:, 0], gate_weight[0], up_weight[0], down_weight[0], rows_avg)
    return (factor[None], product[None])


def solution(mesh):
    placed = (
        P(("expert", "dp"), None),
        P(("expert", "dp"), None),
        P("expert", "dp", None),
        P("expert", "dp", None),
        P("expert", None, "dp"),
    )
    return jax.shard_map(
        on_device,
        mesh=mesh,
        in_specs=placed,
        out_specs=(P("expert", "dp", None), P("expert", None, "dp")),
        check_vma=False,
    )
```
